128 devices in a mesh: lat: 8 (over x_lo, z), lon: 16 (over y, x_hi, core).
Axes of the slice: x: 4 (x_hi: 2, x_lo: 2; x = x_hi * 2 + x_lo), y: 4, z: 4, core: 2. Of those that a mesh axis runs over, the one named last changes fastest.
Arguments:
- features: bfloat16 [65536, 64], P(('lat', 'lon')), may hold values from -6 to 6
- land_tile: int32 [65536, 1], P(('lat', 'lon')), may hold values from 0 to 127; in each aligned block of 512 rows (0 to 511, 512 to 1023, ...) at most 8 rows name the same one
- land_spot: int32 [65536], P(('lat', 'lon')), may hold values from 0 to 1023
- w_in: bfloat16 [64, 256], replicated, may hold values from -0.75 to 0.75
- b_in: float32 [256], replicated, may hold values from -3 to 3
- w_mid: bfloat16 [256, 256], replicated, may hold values from -0.375 to 0.375
- b_mid: float32 [256], replicated, may hold values from -3 to 3
- w_out: bfloat16 [256, 16], replicated, may hold values from -0.375 to 0.375
- tracers: float32 [16, 16, 64, 2048], P(None, None, 'lat', 'lon'), may hold values from -6 to 6
- zonal_wind: float32 [16, 64, 2048], P(None, 'lat', 'lon'), may hold values from -0.95 to 0.95
- meridional_wind: float32 [16, 64, 2048], P(None, 'lat', 'lon'), may hold values from -0.95 to 0.95
- mixing: float32 [64, 16, 16], P('lat'), may hold values from 0 to 0.8, as said below
Outputs:
- tracers_out: float32 [16, 16, 64, 2048], P(None, None, 'lat', 'lon')
The draws below stay inside these ranges and needn't reach their ends.
Inputs may be any that keep to these rules, and one draw needn't show every extreme that they name: `land_tile`: in each aligned block of 512 rows (the land cells of one device), no tile is named by more than 8 rows, a bound that some block reaches; every tile is named somewhere. `mixing`: entries are nonnegative.
All inputs are finite; a program needn't handle non-finite values.
Results may differ from the reference program's by a relative error of at most 0.00044.
Values sent between devices are 32-bit elements; how exact they have to be, the bound alone decides.
No kernel may reach another device: no remote copies, remote signals or barrier semaphores. Data moves between devices by JAX's collectives and lax.ppermute only.
A program may use at most 64 MiB of HBM per device.

```python
import math
import jax
import jax.numpy as jnp
import numpy as np
from jax import lax

TR = 16
LEV = 16
FEAT = 64
HID = 256
SUBSTEPS = 2
LAND_DEV = 512
CLAT = 8
CLON = 128
CAP = 8
LAND = 65536
NLAT = 64
NLON = 2048
N_LON = 16
DEVICES = 128


def draw_mixing(key, part):
    key_diag = jax.random.fold_in(key, 11)
    key_off = jax.random.fold_in(key, 12)
    diag_part = jax.random.uniform(key_diag, (NLAT, LEV), jnp.float32, 0.5, 0.8)
    off_part = jax.random.uniform(key_off, (NLAT, LEV, LEV), jnp.float32, 0.0, 1.0) * (0.5 / LEV)
    identity = jnp.eye(LEV, dtype=jnp.float32)
    return off_part * (1.0 - identity)[None] + diag_part[:, :, None] * identity[None]


def touch_ends(array, rng, low, top_value):
    extent = array.shape
    place = [jax.random.randint(jax.random.fold_in(rng, axis), (), 0, extent[axis]) for axis in range(len(extent))]
    array = array.at[tuple(place)].set(low)
    longest = extent.index(max(extent))
    place[longest] = (place[longest] + 1) % extent[longest]
    return array.at[tuple(place)].set(top_value)


def level_of(key, extent, cuts, low, largest):
    def one(dim, shards_of):
        steps = jax.random.uniform(jax.random.fold_in(jax.random.fold_in(key, 6), dim), (shards_of,), jnp.float32, low / len(cuts), largest / len(cuts))
        return jnp.repeat(jnp.exp(steps), extent[dim] // shards_of).reshape((-1,) + (1,) * (len(extent) - dim - 1))

    level = one(*cuts[0])
    for cut in cuts[1:]:
        level = level * one(*cut)
    return level


def shared_out(stream_key, own, number, rows, number_of, top, limit, lean):
    ranking = jax.random.permutation(stream_key, number_of)
    crowded, usual = shares(number_of, rows * top, limit, lean, True), shares(number_of, rows * top, limit, lean, False)
    places = jnp.arange(number_of)

    def named(tallies, offset_by):
        used = int((tallies > 0).sum())
        fixed = max(1, used // 4)
        shifted = fixed + (places - fixed + offset_by * (used - fixed)) % max(1, number_of - fixed)
        return jnp.zeros((number_of,), jnp.int32).at[ranking[jnp.where(places < fixed, places, shifted)]].set(jnp.asarray(tallies, jnp.int32))

    tallies = jnp.where(number % 4 == 0, named(crowded, number // 4), named(usual, number - number // 4 - 1))
    mixed = jax.random.permutation(jax.random.fold_in(own, 3), number_of)
    source_of, sink = mixed[0:number_of // 2 * 2:2], mixed[1:number_of // 2 * 2:2]
    margin = jnp.minimum(tallies[source_of] - 1, limit - tallies[sink]) // 2
    margin = jnp.where((source_of == ranking[0]) | (sink == ranking[0]) | (tallies[sink] == 0), 0, jnp.maximum(margin, 0))
    shifted = jax.random.randint(jax.random.fold_in(own, 4), (number_of // 2,), 0, 1 << 20) % (margin + 1)
    tallies = tallies.at[source_of].add(-shifted).at[sink].add(shifted)
    labels = jnp.searchsorted(jnp.cumsum(tallies), jnp.arange(rows * top), side="right").astype(jnp.int32)
    grid = labels.reshape(top, rows).T
    grid = grid[jax.random.permutation(jax.random.fold_in(own, 1), rows)]
    offset_by = jax.random.randint(jax.random.fold_in(own, 2), (rows, 1), 0, top)
    return jnp.take_along_axis(grid, (jnp.arange(top)[None, :] + offset_by) % top, axis=1)


def shares(number_of, total, limit, skew, full):
    weights = [(1 << 20) // math.isqrt(grade ** skew) + 1 for grade in range(1, number_of + 1)]
    largest = limit if full else min(limit, max(-(-total // number_of), total * weights[0] // sum(weights)))
    least = 1 if total - largest >= number_of - 1 else 0
    holding, surplus = [largest] + [least] * (number_of - 1), total - largest - least * (number_of - 1)
    while surplus > 0:
        free = [i for i in range(1, number_of) if holding[i] < largest] or [i for i in range(1, number_of) if holding[i] < limit]
        whole, remaining = sum([weights[i] for i in free]), surplus
        for i in free:
            more = min(limit - holding[i], max(1, remaining * weights[i] // whole), surplus)
            holding[i] = holding[i] + more
            surplus = surplus - more
    return np.array(holding)


def centred(rng, dims, spread, most, shards=(), kind=jnp.bfloat16):
    result = spread * jax.random.normal(rng, dims, jnp.float32)
    if shards:
        result = result * level_of(rng, dims, shards, -0.22, 0.18)
    return jnp.clip(result, -most, most).astype(kind)


def setup_inputs(seed: int = 0) -> dict:
    key_of = jax.random.split(jax.random.key(seed), 13)
    features = centred(key_of[0], (LAND, FEAT), 1.0, 6.0, ((0, 128),))
    land_tile_keys = jax.random.split(jax.random.fold_in(key_of[1], 1), LAND // LAND_DEV)
    land_tile_turns = jax.random.permutation(jax.random.fold_in(key_of[1], 3), LAND // LAND_DEV)
    land_tile = jax.vmap(lambda own, number: shared_out(jax.random.fold_in(key_of[1], 2), own, number, LAND_DEV, DEVICES, 1, CAP, 2))(land_tile_keys, land_tile_turns).reshape((LAND, 1))
    land_spot = touch_ends(jax.random.randint(key_of[2], (LAND,), 0, CLAT * CLON), jax.random.fold_in(key_of[2], 1), 0, (CLAT * CLON) - 1).astype(jnp.int32)
    w_in = centred(key_of[3], (FEAT, HID), FEAT ** -0.5, 0.75)
    b_in = centred(key_of[4], (HID,), 0.5, 3.0, (), jnp.float32)
    w_mid = centred(key_of[5], (HID, HID), HID ** -0.5, 0.375)
    b_mid = centred(key_of[6], (HID,), 0.5, 3.0, (), jnp.float32)
    w_out = centred(key_of[7], (HID, TR), HID ** -0.5, 0.375)
    tracers = centred(key_of[8], (TR, LEV, NLAT, NLON), 1.0, 6.0, ((2, 8), (3, 16)), jnp.float32)
    zonal_wind = jnp.clip(jax.random.uniform(key_of[9], (LEV, NLAT, NLON), jnp.float32, -0.95, 0.95) * level_of(key_of[9], (LEV, NLAT, NLON), ((1, 8), (2, 16)), -0.4, 0.0), -0.95, 0.95)
    meridional_wind = jnp.clip(jax.random.uniform(key_of[10], (LEV, NLAT, NLON), jnp.float32, -0.95, 0.95) * level_of(key_of[10], (LEV, NLAT, NLON), ((1, 8), (2, 16)), -0.4, 0.0), -0.95, 0.95)
    mixing = draw_mixing(jax.random.fold_in(key_of[12], 71), 0)
    return dict(features=features, land_tile=land_tile, land_spot=land_spot, w_in=w_in, b_in=b_in, w_mid=w_mid, b_mid=b_mid, w_out=w_out, tracers=tracers, zonal_wind=zonal_wind, meridional_wind=meridional_wind, mixing=mixing)


def section(values, start, stop, axis):
    return lax.slice_in_dim(values, start, values.shape[axis] + stop, axis=axis)


def transport(values, courant, axis):
    edges = 7.0 / 12.0 * (section(values, 1, -2, axis) + section(values, 2, -1, axis)) - 1.0 / 12.0 * (section(values, 0, -3, axis) + section(values, 3, 0, axis))
    left_edge = section(edges, 0, -1, axis)
    right_edge = section(edges, 1, 0, axis)
    centre = section(values, 2, -2, axis)
    slope = right_edge - left_edge
    curve = 6.0 * (centre - 0.5 * (left_edge + right_edge))
    face_courant = section(courant, 2, -3, axis)
    upwind = face_courant * (section(right_edge, 0, -1, axis) - 0.5 * face_courant * (section(slope, 0, -1, axis) - (1.0 - 2.0 / 3.0 * face_courant) * section(curve, 0, -1, axis)))
    reverse = -face_courant
    backward = face_courant * (section(left_edge, 1, 0, axis) + 0.5 * reverse * (section(slope, 1, 0, axis) + (1.0 - 2.0 / 3.0 * reverse) * section(curve, 1, 0, axis)))
    crossing = jnp.where(face_courant >= 0, upwind, backward)
    return section(values, 3, -3, axis) - (section(crossing, 1, 0, axis) - section(crossing, 0, -1, axis))


def wrap_lon(values):
    return jnp.concatenate([values[..., -3:], values, values[..., :3]], axis=3)


def pad_lat(values):
    return jnp.pad(values, ((0, 0), (0, 0), (3, 3), (0, 0)))


def reference(features, land_tile, land_spot, w_in, b_in, w_mid, b_mid, w_out, tracers, zonal_wind, meridional_wind, mixing):
    first = jax.nn.silu(jnp.dot(features, w_in, preferred_element_type=jnp.float32) + b_in).astype(jnp.bfloat16)
    second = jax.nn.silu(jnp.dot(first, w_mid, preferred_element_type=jnp.float32) + b_mid).astype(jnp.bfloat16)
    surface_flux = jnp.dot(second, w_out, preferred_element_type=jnp.float32)
    owner_tile = land_tile[:, 0].astype(jnp.int32)
    spot_index = land_spot.astype(jnp.int32)
    grid_rows = (owner_tile // N_LON) * CLAT + spot_index // CLON
    grid_cols = (owner_tile % N_LON) * CLON + spot_index % CLON
    emitted = jnp.zeros((TR, NLAT, NLON), jnp.float32).at[:, grid_rows, grid_cols].add(surface_flux.T)
    northern = (jnp.arange(NLAT) < NLAT - 1).astype(jnp.float32)
    meridional = (meridional_wind * northern[None, :, None])[None]
    zonal = zonal_wind[None]
    zonal_wide = wrap_lon(zonal)
    meridional_wide = pad_lat(meridional)

    def column(pair):
        state, source = pair
        state = state.at[0].add(source)[None]
        for substep in range(SUBSTEPS):
            state = transport(wrap_lon(state), zonal_wide, 3)
        for substep in range(SUBSTEPS):
            state = transport(pad_lat(state), meridional_wide, 2)
        return jnp.einsum('akj,jab->kab', mixing, state[0], precision=lax.Precision.HIGHEST)

    return lax.map(column, (tracers, emitted))
```

```python
import jax
import jax.numpy as jnp
from jax import lax
from jax.experimental import pallas as pl
from jax.experimental.pallas import tpu as pltpu
from jax.sharding import PartitionSpec as P

F32 = jnp.float32
BF16 = jnp.bfloat16
NT = (((1,), (1,)), ((), ()))
TN = (((0,), (0,)), ((), ()))
ROWS = 10
LATMSG = 17 * 12 + 2
VM = pltpu.VMEM
PARAMS = pltpu.CompilerParams(vmem_limit_bytes=48 * 1024 * 1024)


def vspec():
    return pl.BlockSpec(memory_space=VM)


def sspec():
    return pl.BlockSpec(memory_space=pltpu.SMEM)


def iota(shape, dim):
    return lax.broadcasted_iota(jnp.int32, shape, dim)


def face_weights(c):
    pos = c >= 0
    w = jnp.abs(c)
    al = 0.5 * w * w
    be = 3.0 * al - 2.0 * al * w
    p = w - al - be
    g = al - be
    h = 2.0 * be
    p = jnp.where(pos, p, -p)
    zero = jnp.zeros_like(c)
    gp = jnp.where(pos, g, zero)
    gm = jnp.where(pos, zero, -g)
    hp = jnp.where(pos, h, zero)
    hm = jnp.where(pos, zero, -h)
    a, b = 7.0 / 12.0, 1.0 / 12.0
    return [
        -b * gp,
        a * gp - b * p,
        a * (p + gp) - b * gm + hp,
        a * (p + gm) - b * gp + hm,
        a * gm - b * p,
        -b * gm,
    ]


def step_weights(f, f_before):
    out = []
    for m in range(-3, 4):
        v = None
        if m <= 2:
            v = f_before[m + 3]
        if m >= -2:
            v = -f[m + 2] if v is None else v - f[m + 2]
        if m == 0:
            v = v + 1.0
        out.append(v)
    return out


def shifted(q, low, high, s, axis, pos):
    n = q.shape[axis]
    if s == 0:
        return q
    if s > 0:
        return pltpu.roll(jnp.where(pos < s, high, q), n - s, axis)
    return pltpu.roll(jnp.where(pos >= n + s, low, q), -s, axis)


def double_weights(w, w_low, w_high, axis, pos):
    out = [None] * 13
    for a in range(-3, 4):
        for b in range(-3, 4):
            v = w[a + 3] * shifted(w[b + 3], w_low[b + 3], w_high[b + 3], a, axis, pos)
            out[a + b + 6] = v if out[a + b + 6] is None else out[a + b + 6] + v
    return out


def apply13(v, q, low, high, axis, pos):
    out = v[6] * q
    for s in range(1, 7):
        out = out + v[6 + s] * shifted(q, low, high, s, axis, pos)
        out = out + v[6 - s] * shifted(q, low, high, -s, axis, pos)
    return out


def lon_weights(c, c_halo, lane):
    f, fh = face_weights(c), face_weights(c_halo)
    before = [shifted(x, y, y, -1, 1, lane) for x, y in zip(f, fh)]
    halo_before = [shifted(y, x, x, -1, 1, lane) for x, y in zip(f, fh)]
    w, wh = step_weights(f, before), step_weights(fh, halo_before)
    return double_weights(w, wh, wh, 1, lane)


def lat_weights(c, low, high, sub):
    f, fl, fh = face_weights(c), face_weights(low), face_weights(high)
    before = [shifted(x, y, y, -1, 0, sub) for x, y in zip(f, fl)]
    low_before = [shifted(y, y, y, -1, 0, sub) for y in fl]
    high_before = [shifted(y, x, x, -1, 0, sub) for x, y in zip(f, fh)]
    w = step_weights(f, before)
    wl = step_weights(fl, low_before)
    wh = step_weights(fh, high_before)
    return double_weights(w, wl, wh, 0, sub)


def pack_kernel(ids, tracers, zonal, out_a, out_b):
    odd = (ids[1] & 1) == 1
    slot = iota((8, 128), 1) >> 3

    def pack(read):
        left = right = jnp.zeros((8, 128), F32)
        for k in range(16):
            q = read(k)
            r = q if k == 0 else pltpu.roll(q, 8 * k, 1)
            left = jnp.where(slot == k, r, left)
            right = jnp.where(slot == (k + 15) % 16, r, right)
        return jnp.where(odd, left, right), jnp.where(odd, right, left)

    def body(t, carry):
        a, b = pack(lambda k: tracers[t, k])
        out_a[t], out_b[t] = a, b
        return carry

    lax.fori_loop(0, 16, body, 0)
    a, b = pack(lambda k: zonal[k])
    out_a[16], out_b[16] = a, b


def flux_kernel(feat, tile, spot, w_in, b_in, w_mid, b_mid, w_out, out):
    def silu(v):
        return (v / (1.0 + jnp.exp(-v))).astype(BF16)

    first = silu(lax.dot_general(feat[...], w_in[...], TN, preferred_element_type=F32) + b_in[...])
    second = silu(jnp.dot(first, w_mid[...], preferred_element_type=F32) + b_mid[...])
    flux = lax.dot_general(w_out[...], second, NT, preferred_element_type=F32)
    cells = flux.shape[1]
    member = iota((128, cells), 0) == tile[...]
    member32 = jnp.where(member, 1.0, 0.0)
    member16 = member32.astype(BF16)
    upper = jnp.where(iota((cells, cells), 0) < iota((cells, cells), 1), 1.0, 0.0).astype(BF16)
    earlier = jnp.dot(member16, upper, preferred_element_type=F32)
    slot = jnp.sum(member32 * earlier, axis=0, keepdims=True).astype(jnp.int32)
    high = flux.astype(BF16).astype(F32)
    low = flux - high
    zero = jnp.zeros_like(flux)
    rows_high = jnp.concatenate([jnp.where(slot == s, high, zero) for s in range(8)], 0)
    rows_low = jnp.concatenate([jnp.where(slot == s, low, zero) for s in range(8)], 0)
    sent = lax.dot_general(
        member16, rows_high.astype(BF16), NT, preferred_element_type=F32
    ) + lax.dot_general(member16, rows_low.astype(BF16), NT, preferred_element_type=F32)
    here = (iota((128, cells), 0) & 7) == slot
    places = spot[...]
    coarse = jnp.where(here, (places >> 4) << 4, 0).astype(F32).astype(BF16)
    fine = jnp.where(here, places & 15, 0).astype(F32).astype(BF16)
    spots = lax.dot_general(member16, coarse, NT, preferred_element_type=F32) + lax.dot_general(
        member16, fine, NT, preferred_element_type=F32
    )
    row = iota((128, 128), 0)
    group = iota((128, 128), 1) >> 3

    def beside(x, dn):
        if dn == 0:
            return x
        if dn == 1:
            return jnp.where((row & 15) == 15, pltpu.roll(x, 15, 0), pltpu.roll(x, 127, 0))
        return jnp.where((row & 15) == 0, pltpu.roll(x, 113, 0), pltpu.roll(x, 1, 0))

    def above(x, dl):
        pad = jnp.zeros((16, 128), F32)
        if dl == 0:
            return x
        if dl == 1:
            return jnp.concatenate([x[16:], pad], 0)
        return jnp.concatenate([pad, x[:-16]], 0)

    places_out = jnp.zeros((128, 128), F32)
    for dn in (-1, 0, 1):
        x, y = beside(sent, dn), beside(spots, dn)
        for dl in (-1, 0, 1):
            b = (dl + 1) * 3 + dn + 1
            out[pl.ds(b, 128, stride=ROWS), :] = above(x, dl)
            places_out = jnp.where(group == b, above(y, dl), places_out)
    out[pl.ds(9, 128, stride=ROWS), :] = places_out


def lon_kernel(ids, tracers, zonal, merid, halo_a, halo_b, state, out_a, out_b):
    odd = (ids[1] & 1) == 1
    odd_lat = (ids[0] & 1) == 1
    lane = iota((8, 128), 1)
    slot = lane >> 3
    sub = iota((8, 128), 0)

    def halo(t, k):
        a, b = halo_a[t], halo_b[t]
        right, left = jnp.where(odd, b, a), jnp.where(odd, a, b)
        return pltpu.roll(jnp.where(slot == k, right, left), (128 - 8 * k) & 127, 1)

    def level(k, carry):
        v = lon_weights(zonal[k], halo(16, k), lane)
        for t in range(16):
            h = halo(t, k)
            state[t, k] = apply13(v, tracers[t, k], h, h, 1, lane)
        return carry

    lax.fori_loop(0, 16, level, 0)

    def emit(n, up, down):
        out_a[n] = jnp.where(odd_lat, down, up)
        out_b[n] = jnp.where(odd_lat, up, down)

    def pack(t, read):
        for g in range(4):
            q = [read(4 * g + i) for i in range(4)]
            for i in range(3):
                last = pltpu.roll(q[3], 6 - 2 * i, 0)
                emit(t * 12 + g * 3 + i, jnp.where(sub >= 2, q[i], last), jnp.where(sub < 6, q[i], last))

    def body(t, carry):
        pack(t, lambda k: state[t, k])
        return carry

    lax.fori_loop(0, 16, body, 0)
    keep = jnp.logical_or(sub < 7, ids[0] < 7)
    pack(16, lambda k: jnp.where(keep, merid[k], 0.0))
    emit(204, zonal[0], zonal[0])
    h = halo(16, 0)
    emit(205, h, h)


def lat_kernel(ids, state, zonal, merid, halo_a, halo_b, zonal_halo_a, zonal_halo_b, mixing, out, lonw, latw, column, swept):
    odd_lat = (ids[0] & 1) == 1
    odd = (ids[1] & 1) == 1
    lane = iota((8, 128), 1)
    sub = iota((8, 128), 0)
    keep = jnp.logical_or(sub < 7, ids[0] < 7)

    def message(n):
        a, b = halo_a[n], halo_b[n]
        return jnp.where(odd_lat, a, b), jnp.where(odd_lat, b, a)

    def four(t, g):
        got = [message(t * 12 + g * 3 + i) for i in range(3)]
        pairs = list(got)
        rolled = [[pltpu.roll(got[i][j], 2 + 2 * i, 0) for i in range(3)] for j in range(2)]
        low = jnp.where(sub < 4, rolled[0][0], jnp.where(sub < 6, rolled[0][1], rolled[0][2]))
        high = jnp.where(sub < 2, rolled[1][0], jnp.where(sub < 4, rolled[1][1], rolled[1][2]))
        pairs.append((low, high))
        return pairs

    def group(g, carry):
        winds = four(16, g)
        weights = [
            lat_weights(jnp.where(keep, merid[4 * g + i], 0.0), winds[i][0], winds[i][1], sub)
            for i in range(4)
        ]

        for i in range(4):
            for m in range(13):
                latw[4 * g + i, m] = weights[i][m]

        def tracer(t, c):
            halos = four(t, g)
            for i in range(4):
                v = [latw[4 * g + i, m] for m in range(13)]
                swept[t, pl.ds(32 * g + 8 * i, 8), :] = apply13(
                    v, state[t, 4 * g + i], halos[i][0], halos[i][1], 0, sub
                )
            return c

        return lax.fori_loop(0, 16, tracer, carry)

    lax.fori_loop(0, 4, group, 0)
    slot = lane >> 3
    a, b = zonal_halo_a[16], zonal_halo_b[16]
    own = jnp.where(slot == 0, jnp.where(odd, b, a), jnp.where(odd, a, b))
    wind, wind_halo = message(204), message(205)
    for n, (c, h) in enumerate(((wind[0], wind_halo[0]), (zonal[0], own), (wind[1], wind_halo[1]))):
        v = lon_weights(c, h, lane)
        for m in range(13):
            lonw[n, m] = v[m]
    hi = lax.Precision.HIGHEST
    i, j = iota((128, 128), 0), iota((128, 128), 1)
    order = jnp.where(((i & 7) * 16 + (i >> 3)) == j, 1.0, 0.0)
    by_level = jnp.dot(order, mixing[...], precision=hi, preferred_element_type=F32)
    spread = jnp.where((iota((16, 128), 1) >> 3) == iota((16, 128), 0), 1.0, 0.0)
    matrix = jnp.dot(by_level, spread, precision=hi, preferred_element_type=F32)
    matrix = jnp.where((i & 7) == (j & 7), matrix, 0.0)
    column[...] = jnp.broadcast_to(by_level[:, 0:1], (128, 128))

    def mix(t, carry):
        out[t] = jnp.dot(matrix, swept[t], precision=hi, preferred_element_type=F32)
        return carry

    lax.fori_loop(0, 16, mix, 0)


def emit_kernel(got, mixed, lonw, latw, column, out, grid):
    lane = iota((8, 128), 1)
    sub = iota((8, 128), 0)
    spots = got[pl.ds(9, 128, stride=ROWS), :].T.astype(jnp.int32)
    row_of, col_of = spots >> 7, spots & 127

    def operands(b):
        x = got[pl.ds(b, 128, stride=ROWS), :].T
        high = x.astype(BF16).astype(F32)
        low = x - high
        highs, lows = [], []
        for s in range(8):
            here = row_of[8 * b + s : 8 * b + s + 1, :] == sub

            def spread(y):
                y = jnp.broadcast_to(y[16 * s : 16 * s + 16][:, None, :], (16, 8, 128))
                return jnp.where(here[None], y, 0.0).reshape(128, 128).astype(BF16)

            highs.append(spread(high))
            lows.append(spread(low))
        return jnp.concatenate(highs, 1), jnp.concatenate(lows, 1)

    def columns(b, first, count):
        target = iota((count, 128), 0) + first
        parts = [
            jnp.where(col_of[8 * b + s : 8 * b + s + 1, :] == target, 1.0, 0.0) for s in range(8)
        ]
        whole = jnp.concatenate(parts, 1)
        pieces = []
        if first:
            pieces.append(jnp.zeros((first, 1024), F32))
        pieces.append(whole)
        if first + count < 128:
            pieces.append(jnp.zeros((128 - first - count, 1024), F32))
        return jnp.concatenate(pieces, 0).astype(BF16) if len(pieces) > 1 else whole.astype(BF16)

    def place(b, first, count):
        high, low = operands(b)
        where = columns(b, first, count)
        return lax.dot_general(high, where, NT, preferred_element_type=F32) + lax.dot_general(
            low, where, NT, preferred_element_type=F32
        )

    for n in range(3):
        grid[n, 0] = place(3 * n + 1, 0, 128)
        grid[n, 1] = place(3 * n, 120, 8) + place(3 * n + 2, 0, 8)

    def tracer(t, carry):
        rows = pl.ds(8 * t, 8)
        swept = []
        for n in range(3):
            v = [lonw[n, m] for m in range(13)]
            h = grid[n, 1, rows, :]
            swept.append(apply13(v, grid[n, 0, rows, :], h, h, 1, lane))
        v = [latw[0, m] for m in range(13)]
        e = apply13(v, swept[1], swept[0], swept[2], 0, sub)
        for k in range(16):
            out[t, k] = mixed[t, pl.ds(8 * k, 8), :] + column[pl.ds(8 * k, 8), :] * e
        return carry

    lax.fori_loop(0, 16, tracer, 0)


def call(kernel, ins, outs, scratch=(), smem=0, cost=None):
    return pl.pallas_call(
        kernel,
        out_shape=[jax.ShapeDtypeStruct(s, F32) for s in outs],
        in_specs=[sspec()] * smem + [vspec()] * (len(ins) - smem),
        out_specs=[vspec()] * len(outs),
        scratch_shapes=[VM(s, F32) for s in scratch],
        compiler_params=PARAMS,
        cost_estimate=cost,
    )(*ins)


def pairs(count, first):
    out = []
    for i in range(first, count - 1 + first, 2):
        j = (i + 1) % count
        if j > i or first == 1:
            out += [(i, j), (j, i)]
    return out


def on_device(
    features, land_tile, land_spot, w_in, b_in, w_mid, b_mid, w_out, tracers, zonal_wind, meridional_wind, mixing
):
    ids = jnp.stack([lax.axis_index("lat"), lax.axis_index("lon")]).astype(jnp.int32)
    pack_a, pack_b = call(pack_kernel, (ids, tracers, zonal_wind), [(17, 8, 128)] * 2, smem=1)
    lon_a = [(i, i ^ 1) for i in range(16)]
    lon_b = [(i, (i + 1) % 16 if i & 1 else (i - 1) % 16) for i in range(16)]
    lat_a = [(i, i ^ 1) for i in range(8)]
    lat_b = [(i, i + 1 if i & 1 else i - 1) for i in range(1, 7)]
    halo_b = lax.ppermute(pack_b, "lon", lon_b)
    halo_a = lax.ppermute(pack_a, "lon", lon_a)
    cells = features.shape[0]
    (message,) = call(
        flux_kernel,
        (
            features.T,
            land_tile.reshape(1, cells),
            land_spot.reshape(1, cells),
            w_in,
            b_in.reshape(1, -1),
            w_mid,
            b_mid.reshape(1, -1),
            w_out.T,
        ),
        [(128 * ROWS, 128)],
    )
    got = lax.all_to_all(
        message.reshape(128, 1, ROWS * 128), ("lat", "lon"), split_axis=0, concat_axis=0, tiled=True
    ).reshape(128 * ROWS, 128)
    state, row_a, row_b = call(
        lon_kernel,
        (ids, tracers, zonal_wind, meridional_wind, halo_a, halo_b),
        [(16, 16, 8, 128), (LATMSG, 8, 128), (LATMSG, 8, 128)],
        smem=1,
    )
    rows_a = lax.ppermute(row_a, "lat", lat_a)
    rows_b = lax.ppermute(row_b, "lat", lat_b)
    mixed, lonw, latw, column = call(
        lat_kernel,
        (
            ids,
            state,
            zonal_wind,
            meridional_wind,
            rows_a,
            rows_b,
            halo_a,
            halo_b,
            mixing.reshape(128, 16),
        ),
        [(16, 128, 128), (3, 13, 8, 128), (16, 13, 8, 128), (128, 128)],
        scratch=[(16, 128, 128)],
        smem=1,
    )
    (out,) = call(
        emit_kernel,
        (got, mixed, lonw, latw, column),
        [(16, 16, 8, 128)],
        scratch=[(3, 2, 128, 128)],
    )
    return out


def solution(mesh):
    placed = (
        P(("lat", "lon"), None),
        P(("lat", "lon"), None),
        P(("lat", "lon")),
        P(),
        P(),
        P(),
        P(),
        P(),
        P(None, None, "lat", "lon"),
        P(None, "lat", "lon"),
        P(None, "lat", "lon"),
        P("lat", None, None),
    )
    return jax.shard_map(
        on_device,
        mesh=mesh,
        in_specs=placed,
        out_specs=P(None, None, "lat", "lon"),
        check_vma=False,
    )
```

```python
import jax
import jax.numpy as jnp
from jax import lax
from jax.experimental import pallas as pl
from jax.experimental.pallas import tpu as pltpu
from jax.sharding import PartitionSpec as P

F32 = jnp.float32
BF16 = jnp.bfloat16
NT = (((1,), (1,)), ((), ()))
TN = (((0,), (0,)), ((), ()))
ROWS = 10
LATMSG = 17 * 12 + 3
VM = pltpu.VMEM
PARAMS = pltpu.CompilerParams(vmem_limit_bytes=12 * 1024 * 1024)


def vspec():
    return pl.BlockSpec(memory_space=VM)


def iota(shape, dim):
    return lax.broadcasted_iota(jnp.int32, shape, dim)


def face_weights(c):
    pos = c >= 0
    w = jnp.abs(c)
    al = 0.5 * w * w
    be = 3.0 * al - 2.0 * al * w
    p = w - al - be
    g = al - be
    h = 2.0 * be
    p = jnp.where(pos, p, -p)
    zero = jnp.zeros_like(c)
    gp = jnp.where(pos, g, zero)
    gm = jnp.where(pos, zero, -g)
    hp = jnp.where(pos, h, zero)
    hm = jnp.where(pos, zero, -h)
    a, b = 7.0 / 12.0, 1.0 / 12.0
    return [
        -b * gp,
        a * gp - b * p,
        a * (p + gp) - b * gm + hp,
        a * (p + gm) - b * gp + hm,
        a * gm - b * p,
        -b * gm,
    ]


def step_weights(f, f_before):
    out = []
    for m in range(-3, 4):
        v = None
        if m <= 2:
            v = f_before[m + 3]
        if m >= -2:
            v = -f[m + 2] if v is None else v - f[m + 2]
        if m == 0:
            v = v + 1.0
        out.append(v)
    return out


def shifted(q, low, high, s, axis, pos):
    n = q.shape[axis]
    if s == 0:
        return q
    if s > 0:
        return pltpu.roll(jnp.where(pos < s, high, q), n - s, axis)
    return pltpu.roll(jnp.where(pos >= n + s, low, q), -s, axis)


def double_weights(w, w_low, w_high, axis, pos):
    out = [None] * 13
    for a in range(-3, 4):
        for b in range(-3, 4):
            v = w[a + 3] * shifted(w[b + 3], w_low[b + 3], w_high[b + 3], a, axis, pos)
            out[a + b + 6] = v if out[a + b + 6] is None else out[a + b + 6] + v
    return out


def zonal_weights(wind, out):
    def block(b, carry):
        f = face_weights(wind[pl.ds(8 * b + 5, 8), :])
        before = face_weights(wind[pl.ds(8 * b + 4, 8), :])
        for m, w in enumerate(step_weights(f, before)):
            out[m, pl.ds(pl.multiple_of(8 * b, 8), 8), :] = w
        return carry

    lax.fori_loop(0, 17, block, 0)


def zonal_steps_unrolled(weights, first, second):
    def total(terms):
        while len(terms) > 1:
            terms = [x + y for x, y in zip(terms[::2], terms[1::2])] + ([terms[-1]] if len(terms) & 1 else [])
        return terms[0]

    for b in range(17):
        second[8 * b : 8 * b + 8] = total(
            [weights[m, 8 * b : 8 * b + 8, :] * first[8 * b + 2 + m : 8 * b + 10 + m] for m in range(7)]
        )
    for b in range(16):
        first[8 * b + 8 : 8 * b + 16] = total(
            [weights[m, 8 * b + 3 : 8 * b + 11, :] * second[8 * b + m : 8 * b + 8 + m] for m in range(7)]
        )


def zonal_steps(weights, first, second, count):
    def one(b, carry):
        w = [weights[m, pl.ds(pl.multiple_of(8 * b, 8), 8), :] for m in range(7)]
        for t in range(count):
            v = w[0] * first[t, pl.ds(8 * b + 2, 8), :]
            for m in range(1, 7):
                v = v + w[m] * first[t, pl.ds(8 * b + 2 + m, 8), :]
            second[t, pl.ds(pl.multiple_of(8 * b, 8), 8), :] = v
        return carry

    lax.fori_loop(0, 17, one, 0)

    def two(b, carry):
        w = [weights[m, pl.ds(8 * b + 3, 8), :] for m in range(7)]
        for t in range(count):
            v = w[0] * second[t, pl.ds(8 * b, 8), :]
            for m in range(1, 7):
                v = v + w[m] * second[t, pl.ds(8 * b + m, 8), :]
            first[t, pl.ds(pl.multiple_of(8 * b + 8, 8), 8), :] = v
        return carry

    lax.fori_loop(0, 16, two, 0)


def lat_weights(c, low, high, sub):
    f, fl, fh = face_weights(c), face_weights(low), face_weights(high)
    before = [shifted(x, y, y, -1, 0, sub) for x, y in zip(f, fl)]
    low_before = [shifted(y, y, y, -1, 0, sub) for y in fl]
    high_before = [shifted(y, x, x, -1, 0, sub) for x, y in zip(f, fh)]
    w = step_weights(f, before)
    wl = step_weights(fl, low_before)
    wh = step_weights(fh, high_before)
    return double_weights(w, wl, wh, 0, sub)


def pack_kernel(ids, tracers_hbm, zonal_hbm, out_a, out_b, turned, tracers, zonal, sems):
    odd = (ids[1] & 1) == 1
    chunks = [(zonal_hbm, zonal)]
    chunks += [(tracers_hbm.at[pl.ds(4 * n, 4)], tracers.at[pl.ds(4 * n, 4)]) for n in range(4)]
    copies = load(chunks, sems)

    def put(t, x):
        x = x.T
        turned[t] = x
        left, right = x[0:8], x[120:128]
        out_a[t] = jnp.where(odd, left, right)
        out_b[t] = jnp.where(odd, right, left)

    copies[0].wait()
    put(16, zonal[...])
    for n in range(4):
        copies[n + 1].wait()
        for t in range(4 * n, 4 * n + 4):
            put(t, tracers[t])


def flux_kernel(*refs):
    out, sems = refs[8], refs[17]
    feat, tile, spot, w_in, b_in, w_mid, b_mid, w_out = refs[9:17]
    for c in load(list(zip(refs[:8], refs[9:17])), sems):
        c.wait()

    def silu(v):
        return (v / (1.0 + jnp.exp(-v))).astype(BF16)

    first = silu(lax.dot_general(feat[...], w_in[...], TN, preferred_element_type=F32) + b_in[...])
    second = silu(jnp.dot(first, w_mid[...], preferred_element_type=F32) + b_mid[...])
    flux = lax.dot_general(w_out[...], second, NT, preferred_element_type=F32)
    cells = flux.shape[1]
    member = iota((128, cells), 0) == tile[...]
    member32 = jnp.where(member, 1.0, 0.0)
    member16 = member32.astype(BF16)
    upper = jnp.where(iota((cells, cells), 0) < iota((cells, cells), 1), 1.0, 0.0).astype(BF16)
    earlier = jnp.dot(member16, upper, preferred_element_type=F32)
    slot = jnp.sum(member32 * earlier, axis=0, keepdims=True).astype(jnp.int32)
    high = flux.astype(BF16).astype(F32)
    low = flux - high
    zero = jnp.zeros_like(flux)
    rows_high = jnp.concatenate([jnp.where(slot == s, high, zero) for s in range(8)], 0)
    rows_low = jnp.concatenate([jnp.where(slot == s, low, zero) for s in range(8)], 0)
    sent = lax.dot_general(
        member16, rows_high.astype(BF16), NT, preferred_element_type=F32
    ) + lax.dot_general(member16, rows_low.astype(BF16), NT, preferred_element_type=F32)
    here = (iota((128, cells), 0) & 7) == slot
    places = spot[...]
    coarse = jnp.where(here, (places >> 4) << 4, 0).astype(F32).astype(BF16)
    fine = jnp.where(here, places & 15, 0).astype(F32).astype(BF16)
    spots = lax.dot_general(member16, coarse, NT, preferred_element_type=F32) + lax.dot_general(
        member16, fine, NT, preferred_element_type=F32
    )
    row = iota((128, 128), 0)
    group = iota((128, 128), 1) >> 3

    def beside(x, dn):
        if dn == 0:
            return x
        if dn == 1:
            return jnp.where((row & 15) == 15, pltpu.roll(x, 15, 0), pltpu.roll(x, 127, 0))
        return jnp.where((row & 15) == 0, pltpu.roll(x, 113, 0), pltpu.roll(x, 1, 0))

    def above(x, dl):
        pad = jnp.zeros((16, 128), F32)
        if dl == 0:
            return x
        if dl == 1:
            return jnp.concatenate([x[16:], pad], 0)
        return jnp.concatenate([pad, x[:-16]], 0)

    places_out = jnp.zeros((128, 128), F32)
    for dn in (-1, 0, 1):
        x, y = beside(sent, dn), beside(spots, dn)
        for dl in (-1, 0, 1):
            b = (dl + 1) * 3 + dn + 1
            out[pl.ds(b, 128, stride=ROWS), :] = above(x, dl)
            places_out = jnp.where(group == b, above(y, dl), places_out)
    out[pl.ds(9, 128, stride=ROWS), :] = places_out


def lon_kernel(
    ids, turned, zonal, merid_hbm, halo_a, halo_b, state, out_a, out_b, wind, weights, first, second, merid, surface, sems
):
    copies = load([(merid_hbm, merid), (zonal.at[pl.ds(0, 8)], surface)], sems)
    odd = (ids[1] & 1) == 1
    odd_lat = (ids[0] & 1) == 1
    sub = iota((8, 128), 0)

    def halo(t):
        a, b = halo_a[t], halo_b[t]
        return jnp.where(odd, a, b), jnp.where(odd, b, a)

    left, right = halo(16)
    wind[0:8], wind[8:136], wind[136:144] = left, turned[16], right
    zonal_weights(wind, weights)
    for t in range(16):
        low, high = halo(t)
        first[t, 0:8], first[t, 8:136], first[t, 136:144] = low, turned[t], high
    zonal_steps(weights, first, second, 16)
    for t in range(16):
        state[t] = first[t, 8:136].T

    def emit(n, up, down):
        out_a[n] = jnp.where(odd_lat, down, up)
        out_b[n] = jnp.where(odd_lat, up, down)

    def pack(t, read):
        for g in range(4):
            q = [read(4 * g + i) for i in range(4)]
            for i in range(3):
                last = pltpu.roll(q[3], 6 - 2 * i, 0)
                emit(t * 12 + g * 3 + i, jnp.where(sub >= 2, q[i], last), jnp.where(sub < 6, q[i], last))

    def body(t, carry):
        pack(t, lambda k: state[t, 8 * k : 8 * k + 8, :])
        return carry

    lax.fori_loop(0, 16, body, 0)
    keep = jnp.logical_or(sub < 7, ids[0] < 7)
    for c in copies:
        c.wait()
    pack(16, lambda k: jnp.where(keep, merid[k], 0.0))
    emit(204, surface[...], surface[...])
    emit(205, left, left)
    emit(206, right, right)


def lat_kernel(
    ids,
    state,
    merid_hbm,
    a_hbm,
    b_hbm,
    edge,
    mixing_hbm,
    out,
    lonw,
    top,
    column,
    swept,
    wide,
    wind,
    latw,
    merid,
    halo_a,
    halo_b,
    mixing,
    sems,
):
    copies = load([(a_hbm, halo_a), (b_hbm, halo_b), (merid_hbm, merid), (mixing_hbm, mixing)], sems)
    odd_lat = (ids[0] & 1) == 1
    sub = iota((8, 128), 0)
    keep = jnp.logical_or(sub < 7, ids[0] < 7)
    hi = lax.Precision.HIGHEST
    i, j = iota((128, 128), 0), iota((128, 128), 1)

    def message(n):
        a, b = halo_a[n], halo_b[n]
        return jnp.where(odd_lat, a, b), jnp.where(odd_lat, b, a)

    def four(t, g):
        got = [message(t * 12 + g * 3 + x) for x in range(3)]
        rolled = [[pltpu.roll(got[x][y], 2 + 2 * x, 0) for x in range(3)] for y in range(2)]
        low = jnp.where(sub < 4, rolled[0][0], jnp.where(sub < 6, rolled[0][1], rolled[0][2]))
        high = jnp.where(sub < 2, rolled[1][0], jnp.where(sub < 4, rolled[1][1], rolled[1][2]))
        return got + [(low, high)]

    def unpack(t, carry):
        for g in range(4):
            for x, (low, high) in enumerate(four(t, g)):
                k = 4 * g + x
                wide[t, k, 0:8], wide[t, k, 8:16], wide[t, k, 16:24] = low, state[t, 8 * k : 8 * k + 8, :], high
        return carry

    spread = jnp.where((j & 7) == i, 1.0, 0.0)

    def level_zero(n):
        wind[n] = jnp.dot(wind[n], spread, precision=hi, preferred_element_type=F32)
        zonal_weights(wind.at[n], lonw.at[n])

    wind[1] = edge[...]
    level_zero(1)
    copies[3].wait()
    order = jnp.where(((i & 7) * 16 + (i >> 3)) == j, 1.0, 0.0)
    by_level = jnp.dot(order, mixing[...], precision=hi, preferred_element_type=F32)
    expand = jnp.where((iota((16, 128), 1) >> 3) == iota((16, 128), 0), 1.0, 0.0)
    matrix = jnp.dot(by_level, expand, precision=hi, preferred_element_type=F32)
    matrix = jnp.where((i & 7) == (j & 7), matrix, 0.0)
    column[...] = jnp.broadcast_to(by_level[:, 0:1], (128, 128))
    for c in copies[:3]:
        c.wait()
    lax.fori_loop(0, 16, unpack, 0)
    for g in range(4):
        for x, (low, high) in enumerate(four(16, g)):
            k = 4 * g + x
            wide[16, k, 0:8], wide[16, k, 8:16], wide[16, k, 16:24] = low, jnp.where(keep, merid[k], 0.0), high
    centre, left, right = message(204), message(205), message(206)
    for n in (0, 2):
        m = n // 2
        wind[n, 0:8], wind[n, 136:144] = left[m], right[m]
        wind[n, 8:136] = jnp.concatenate([centre[m]] * 16, 0).T
        level_zero(n)

    def level(k, carry):
        v = lat_weights(wide[16, k, 8:16], wide[16, k, 0:8], wide[16, k, 16:24], sub)
        for m in range(13):
            latw[k, m] = v[m]
        for t in range(16):
            q = v[0] * wide[t, k, 2:10]
            for m in range(1, 13):
                q = q + v[m] * wide[t, k, 2 + m : 10 + m]
            swept[t, pl.ds(pl.multiple_of(8 * k, 8), 8), :] = q
        return carry

    lax.fori_loop(0, 16, level, 0)
    top[...] = latw[0]
    for t in range(16):
        out[t] = jnp.dot(matrix, swept[t], precision=hi, preferred_element_type=F32)


def emit_kernel(got, mixed_hbm, lonw, latw, column, out_hbm, grid, second, turned, wide, mixed, out, sems):
    copies = load([(mixed_hbm, mixed)], sems)
    sub = iota((8, 128), 0)
    spots = got[pl.ds(9, 128, stride=ROWS), :].T.astype(jnp.int32)
    row_of, col_of = spots >> 7, spots & 127

    def split(b):
        x = got[pl.ds(b, 128, stride=ROWS), :].T
        high = x.astype(BF16).astype(F32)
        return high, x - high

    def main(b):
        high, low = split(b)
        turned[0], turned[1] = high, low
        highs, lows, where = [], [], []
        target = iota((128, 128), 0)
        for s in range(8):
            here = row_of[8 * b + s : 8 * b + s + 1, :] == sub

            def rows(n):
                return jnp.concatenate(
                    [
                        jnp.where(here, jnp.broadcast_to(turned[n, 16 * s + t : 16 * s + t + 1, :], (8, 128)), 0.0)
                        for t in range(16)
                    ],
                    0,
                ).astype(BF16)

            highs.append(rows(0))
            lows.append(rows(1))
            where.append(jnp.where(col_of[8 * b + s : 8 * b + s + 1, :] == target, 1.0, 0.0).astype(BF16))
        where = jnp.concatenate(where, 1)
        return lax.dot_general(where, jnp.concatenate(highs, 1), NT, preferred_element_type=F32) + lax.dot_general(
            where, jnp.concatenate(lows, 1), NT, preferred_element_type=F32
        )

    expand = jnp.where((iota((32, 128), 0) & 15) == (iota((32, 128), 1) >> 3), 1.0, 0.0)
    diagonal = (iota((64, 128), 0) & 7) == (iota((64, 128), 1) & 7)

    def side(b, first):
        high, low = split(b)
        flux = jnp.concatenate(
            [jnp.concatenate([high[16 * s : 16 * s + 16], low[16 * s : 16 * s + 16]], 0) for s in range(8)], 1
        ).astype(BF16)
        key = (col_of - first) * 8 + row_of
        target = iota((64, 128), 0)
        where = jnp.concatenate(
            [jnp.where(key[8 * b + s : 8 * b + s + 1, :] == target, 1.0, 0.0) for s in range(8)], 1
        ).astype(BF16)
        sums = lax.dot_general(where, flux, NT, preferred_element_type=F32)
        sums = jnp.dot(sums, expand, precision=lax.Precision.HIGHEST, preferred_element_type=F32)
        sums = jnp.where(diagonal, sums, 0.0)
        return jnp.concatenate([jnp.sum(sums[8 * c : 8 * c + 8], 0, keepdims=True) for c in range(8)], 0)

    for n in range(3):
        grid[n, 0:8] = side(3 * n, 120)
        grid[n, 8:136] = main(3 * n + 1)
        grid[n, 136:144] = side(3 * n + 2, 0)
    for n in range(3):
        zonal_steps_unrolled(lonw.at[n], grid.at[n], second.at[n])
    for n in range(3):
        back = grid[n, 8:136].T
        for t in range(16):
            wide[t, 8 * n : 8 * n + 8] = back[8 * t : 8 * t + 8]

    copies[0].wait()

    def tracer(t):
        e = latw[0] * wide[t, 2:10]
        for m in range(1, 13):
            e = e + latw[m] * wide[t, 2 + m : 10 + m]
        for k in range(16):
            out[t, 8 * k : 8 * k + 8] = mixed[t, 8 * k : 8 * k + 8, :] + column[8 * k : 8 * k + 8, :] * e

    stores = []
    for n in range(4):
        for t in range(4 * n, 4 * n + 4):
            tracer(t)
        part = pl.ds(4 * n, 4)
        stores.append(pltpu.make_async_copy(out.at[part], out_hbm.at[part], sems.at[1 + n]))
        stores[-1].start()
    for c in stores:
        c.wait()


def call(kernel, ins, outs, scratch=(), kinds=None, copies=0, out_spec=None):
    spec = {"s": pltpu.SMEM, "v": VM, "h": pltpu.HBM}
    rooms = [VM(x, F32) if isinstance(x, tuple) else x for x in scratch]
    if copies:
        rooms.append(pltpu.SemaphoreType.DMA((copies,)))
    return pl.pallas_call(
        kernel,
        out_shape=[jax.ShapeDtypeStruct(s, F32) for s in outs],
        in_specs=[pl.BlockSpec(memory_space=spec[x]) for x in kinds],
        out_specs=[out_spec or vspec()] * len(outs),
        scratch_shapes=rooms,
        compiler_params=PARAMS,
    )(*[pltpu.with_memory_space_constraint(x, pltpu.HBM) if k == "h" else x for x, k in zip(ins, kinds)])


def load(pairs, sems):
    copies = [pltpu.make_async_copy(x, y, sems.at[n]) for n, (x, y) in enumerate(pairs)]
    for c in copies:
        c.start()
    return copies


def on_device(
    features, land_tile, land_spot, w_in, b_in, w_mid, b_mid, w_out, tracers, zonal_wind, meridional_wind, mixing
):
    ids = jnp.stack([lax.axis_index("lat"), lax.axis_index("lon")]).astype(jnp.int32)
    shape = tracers.shape
    tracers = tracers.reshape(16, 128, 128)
    zonal = zonal_wind.reshape(128, 128)
    pack_a, pack_b, turned = call(
        pack_kernel,
        (ids, tracers, zonal),
        [(17, 8, 128), (17, 8, 128), (17, 128, 128)],
        scratch=[(16, 128, 128), (128, 128)],
        kinds="shh",
        copies=5,
    )
    lon_a = [(i, i ^ 1) for i in range(16)]
    lon_b = [(i, (i + 1) % 16 if i & 1 else (i - 1) % 16) for i in range(16)]
    lat_a = [(i, i ^ 1) for i in range(8)]
    lat_b = [(i, i + 1 if i & 1 else i - 1) for i in range(1, 7)]
    halo_b = lax.ppermute(pack_b, "lon", lon_b)
    halo_a = lax.ppermute(pack_a, "lon", lon_a)
    cells = features.shape[0]
    inputs = (
        features.T,
        land_tile.reshape(1, cells),
        land_spot.reshape(1, cells),
        w_in,
        b_in.reshape(1, -1),
        w_mid,
        b_mid.reshape(1, -1),
        w_out.T,
    )
    (message,) = call(
        flux_kernel,
        inputs,
        [(128 * ROWS, 128)],
        scratch=[VM(x.shape, x.dtype) for x in inputs],
        kinds="h" * 8,
        copies=8,
    )
    halo_a, halo_b, message = lax.optimization_barrier((halo_a, halo_b, message))
    state, row_a, row_b, edge = call(
        lon_kernel,
        (ids, turned, zonal, meridional_wind, halo_a, halo_b),
        [(16, 128, 128), (LATMSG, 8, 128), (LATMSG, 8, 128), (144, 128)],
        scratch=[(7, 136, 128), (16, 144, 128), (16, 136, 128), (16, 8, 128), (8, 128)],
        kinds="svhhvv",
        copies=2,
    )
    rows_a = lax.ppermute(row_a, "lat", lat_a)
    rows_b = lax.ppermute(row_b, "lat", lat_b)
    got = lax.all_to_all(
        message.reshape(128, 1, ROWS * 128), ("lat", "lon"), split_axis=0, concat_axis=0, tiled=True
    ).reshape(128 * ROWS, 128)
    mixed, lonw, latw, column = call(
        lat_kernel,
        (ids, state, meridional_wind, rows_a, rows_b, edge, mixing.reshape(128, 16)),
        [(16, 128, 128), (3, 7, 136, 128), (13, 8, 128), (128, 128)],
        scratch=[
            (16, 128, 128),
            (17, 16, 24, 128),
            (3, 144, 128),
            (16, 13, 8, 128),
            (16, 8, 128),
            (LATMSG, 8, 128),
            (LATMSG, 8, 128),
            (128, 16),
        ],
        kinds="svhhhvh",
        copies=4,
    )
    (out,) = call(
        emit_kernel,
        (got, mixed, lonw, latw, column),
        [(16, 128, 128)],
        scratch=[(3, 144, 128), (3, 136, 128), (2, 128, 128), (16, 24, 128), (16, 128, 128), (16, 128, 128)],
        kinds="vhvvv",
        copies=5,
        out_spec=pl.BlockSpec(memory_space=pl.ANY),
    )
    return out.reshape(shape)


def solution(mesh):
    placed = (
        P(("lat", "lon"), None),
        P(("lat", "lon"), None),
        P(("lat", "lon")),
        P(),
        P(),
        P(),
        P(),
        P(),
        P(None, None, "lat", "lon"),
        P(None, "lat", "lon"),
        P(None, "lat", "lon"),
        P("lat", None, None),
    )
    return jax.shard_map(
        on_device,
        mesh=mesh,
        in_specs=placed,
        out_specs=P(None, None, "lat", "lon"),
        check_vma=False,
    )
```

```python
import jax
import jax.numpy as jnp
from jax import lax
from jax.experimental import pallas as pl
from jax.experimental.pallas import tpu as pltpu
from jax.sharding import PartitionSpec as P

F32 = jnp.float32
BF16 = jnp.bfloat16
NT = (((1,), (1,)), ((), ()))
TN = (((0,), (0,)), ((), ()))
ROWS = 10
N1 = 8
N2 = 16 - N1
WIND = 12 * N1
MSG1 = WIND + 15
MSG2 = 12 * N2
VM = pltpu.VMEM
PARAMS = pltpu.CompilerParams(vmem_limit_bytes=12 * 1024 * 1024)


def vspec():
    return pl.BlockSpec(memory_space=VM)


def iota(shape, dim):
    return lax.broadcasted_iota(jnp.int32, shape, dim)


def face_weights(c):
    pos = c >= 0
    w = jnp.abs(c)
    al = 0.5 * w * w
    be = 3.0 * al - 2.0 * al * w
    p = w - al - be
    g = al - be
    h = 2.0 * be
    p = jnp.where(pos, p, -p)
    zero = jnp.zeros_like(c)
    gp = jnp.where(pos, g, zero)
    gm = jnp.where(pos, zero, -g)
    hp = jnp.where(pos, h, zero)
    hm = jnp.where(pos, zero, -h)
    a, b = 7.0 / 12.0, 1.0 / 12.0
    return [
        -b * gp,
        a * gp - b * p,
        a * (p + gp) - b * gm + hp,
        a * (p + gm) - b * gp + hm,
        a * gm - b * p,
        -b * gm,
    ]


def step_weights(f, f_before):
    out = []
    for m in range(-3, 4):
        v = None
        if m <= 2:
            v = f_before[m + 3]
        if m >= -2:
            v = -f[m + 2] if v is None else v - f[m + 2]
        if m == 0:
            v = v + 1.0
        out.append(v)
    return out


def shifted(q, low, high, s, axis, pos):
    n = q.shape[axis]
    if s == 0:
        return q
    if s > 0:
        return pltpu.roll(jnp.where(pos < s, high, q), n - s, axis)
    return pltpu.roll(jnp.where(pos >= n + s, low, q), -s, axis)


def double_weights(w, w_low, w_high, axis, pos):
    out = [None] * 13
    for a in range(-3, 4):
        for b in range(-3, 4):
            v = w[a + 3] * shifted(w[b + 3], w_low[b + 3], w_high[b + 3], a, axis, pos)
            out[a + b + 6] = v if out[a + b + 6] is None else out[a + b + 6] + v
    return out


def zonal_weights(wind, out):
    for b in range(17):
        f = face_weights(wind[8 * b + 5 : 8 * b + 13])
        before = face_weights(wind[8 * b + 4 : 8 * b + 12])
        for m, w in enumerate(step_weights(f, before)):
            out[m, 8 * b : 8 * b + 8] = w


def zonal_steps_unrolled(weights, first, second):
    def total(terms):
        while len(terms) > 1:
            terms = [x + y for x, y in zip(terms[::2], terms[1::2])] + ([terms[-1]] if len(terms) & 1 else [])
        return terms[0]

    for b in range(17):
        second[8 * b : 8 * b + 8] = total(
            [weights[m, 8 * b : 8 * b + 8, :] * first[8 * b + 2 + m : 8 * b + 10 + m] for m in range(7)]
        )
    for b in range(16):
        first[8 * b + 8 : 8 * b + 16] = total(
            [weights[m, 8 * b + 3 : 8 * b + 11, :] * second[8 * b + m : 8 * b + 8 + m] for m in range(7)]
        )


def zonal_steps(weights, first, second, count):
    def one(b, carry):
        w = [weights[m, pl.ds(pl.multiple_of(8 * b, 8), 8), :] for m in range(7)]
        for t in range(count):
            v = w[0] * first[t, pl.ds(8 * b + 2, 8), :]
            for m in range(1, 7):
                v = v + w[m] * first[t, pl.ds(8 * b + 2 + m, 8), :]
            second[t, pl.ds(pl.multiple_of(8 * b, 8), 8), :] = v
        return carry

    lax.fori_loop(0, 17, one, 0)

    def two(b, carry):
        w = [weights[m, pl.ds(8 * b + 3, 8), :] for m in range(7)]
        for t in range(count):
            v = w[0] * second[t, pl.ds(8 * b, 8), :]
            for m in range(1, 7):
                v = v + w[m] * second[t, pl.ds(8 * b + m, 8), :]
            first[t, pl.ds(pl.multiple_of(8 * b + 8, 8), 8), :] = v
        return carry

    lax.fori_loop(0, 16, two, 0)


def lat_weights(c, low, high, sub):
    f, fl, fh = face_weights(c), face_weights(low), face_weights(high)
    before = [shifted(x, y, y, -1, 0, sub) for x, y in zip(f, fl)]
    low_before = [shifted(y, y, y, -1, 0, sub) for y in fl]
    high_before = [shifted(y, x, x, -1, 0, sub) for x, y in zip(f, fh)]
    w = step_weights(f, before)
    wl = step_weights(fl, low_before)
    wh = step_weights(fh, high_before)
    return double_weights(w, wl, wh, 0, sub)


def pack_kernel(ids, tracers_hbm, zonal_hbm, out_a, out_b, turned, tracers, zonal, sems):
    odd = (ids[1] & 1) == 1
    chunks = [(zonal_hbm, zonal)]
    chunks += [(tracers_hbm.at[pl.ds(4 * n, 4)], tracers.at[pl.ds(4 * n, 4)]) for n in range(4)]
    copies = load(chunks, sems)

    def put(t, x):
        x = x.T
        turned[t] = x
        left, right = x[0:8], x[120:128]
        out_a[t] = jnp.where(odd, left, right)
        out_b[t] = jnp.where(odd, right, left)

    copies[0].wait()
    put(16, zonal[...])
    for n in range(4):
        copies[n + 1].wait()
        for t in range(4 * n, 4 * n + 4):
            put(t, tracers[t])


def flux_kernel(*refs):
    out, sems = refs[8], refs[17]
    feat, tile, spot, w_in, b_in, w_mid, b_mid, w_out = refs[9:17]
    for c in load(list(zip(refs[:8], refs[9:17])), sems):
        c.wait()

    def silu(v):
        return (v / (1.0 + jnp.exp(-v))).astype(BF16)

    first = silu(lax.dot_general(feat[...], w_in[...], TN, preferred_element_type=F32) + b_in[...])
    second = silu(jnp.dot(first, w_mid[...], preferred_element_type=F32) + b_mid[...])
    flux = lax.dot_general(w_out[...], second, NT, preferred_element_type=F32)
    cells = flux.shape[1]
    member = iota((128, cells), 0) == tile[...]
    member32 = jnp.where(member, 1.0, 0.0)
    member16 = member32.astype(BF16)
    upper = jnp.where(iota((cells, cells), 0) < iota((cells, cells), 1), 1.0, 0.0).astype(BF16)
    earlier = jnp.dot(member16, upper, preferred_element_type=F32)
    slot = jnp.sum(member32 * earlier, axis=0, keepdims=True).astype(jnp.int32)
    high = flux.astype(BF16).astype(F32)
    low = flux - high
    zero = jnp.zeros_like(flux)
    rows_high = jnp.concatenate([jnp.where(slot == s, high, zero) for s in range(8)], 0)
    rows_low = jnp.concatenate([jnp.where(slot == s, low, zero) for s in range(8)], 0)
    sent = lax.dot_general(
        member16, rows_high.astype(BF16), NT, preferred_element_type=F32
    ) + lax.dot_general(member16, rows_low.astype(BF16), NT, preferred_element_type=F32)
    here = (iota((128, cells), 0) & 7) == slot
    places = spot[...]
    coarse = jnp.where(here, (places >> 4) << 4, 0).astype(F32).astype(BF16)
    fine = jnp.where(here, places & 15, 0).astype(F32).astype(BF16)
    spots = lax.dot_general(member16, coarse, NT, preferred_element_type=F32) + lax.dot_general(
        member16, fine, NT, preferred_element_type=F32
    )
    row = iota((128, 128), 0)
    group = iota((128, 128), 1) >> 3

    def beside(x, dn):
        if dn == 0:
            return x
        if dn == 1:
            return jnp.where((row & 15) == 15, pltpu.roll(x, 15, 0), pltpu.roll(x, 127, 0))
        return jnp.where((row & 15) == 0, pltpu.roll(x, 113, 0), pltpu.roll(x, 1, 0))

    def above(x, dl):
        pad = jnp.zeros((16, 128), F32)
        if dl == 0:
            return x
        if dl == 1:
            return jnp.concatenate([x[16:], pad], 0)
        return jnp.concatenate([pad, x[:-16]], 0)

    places_out = jnp.zeros((128, 128), F32)
    for dn in (-1, 0, 1):
        x, y = beside(sent, dn), beside(spots, dn)
        for dl in (-1, 0, 1):
            b = (dl + 1) * 3 + dn + 1
            out[pl.ds(b, 128, stride=ROWS), :] = above(x, dl)
            places_out = jnp.where(group == b, above(y, dl), places_out)
    out[pl.ds(9, 128, stride=ROWS), :] = places_out


def sweep_columns(ids, base, count, turned, halo_a, halo_b, state, weights, first, second):
    odd = (ids[1] & 1) == 1
    for t in range(count):
        a, b = halo_a[base + t], halo_b[base + t]
        first[t, 0:8], first[t, 136:144] = jnp.where(odd, a, b), jnp.where(odd, b, a)
        first[t, 8:136] = turned[base + t]
    zonal_steps(weights, first, second, count)
    for t in range(count):
        state[t] = first[t, 8:136].T


def row_packer(ids, out_a, out_b):
    odd_lat = (ids[0] & 1) == 1
    sub = iota((8, 128), 0)

    def emit(n, up, down):
        out_a[n] = jnp.where(odd_lat, down, up)
        out_b[n] = jnp.where(odd_lat, up, down)

    def pack(n, read):
        for g in range(4):
            q = [read(4 * g + i) for i in range(4)]
            for i in range(3):
                last = pltpu.roll(q[3], 6 - 2 * i, 0)
                emit(n + g * 3 + i, jnp.where(sub >= 2, q[i], last), jnp.where(sub < 6, q[i], last))

    return emit, pack


def lon_first_kernel(
    ids, turned, zonal, merid_hbm, halo_a, halo_b, state_hbm, out_a, out_b, wind, weights, first, second, merid, surface, state, sems
):
    copies = load([(merid_hbm, merid), (zonal.at[pl.ds(0, 8)], surface)], sems)
    odd = (ids[1] & 1) == 1
    a, b = halo_a[16], halo_b[16]
    left, right = jnp.where(odd, a, b), jnp.where(odd, b, a)
    wind[0:8], wind[8:136], wind[136:144] = left, turned[16], right
    zonal_weights(wind, weights)
    sweep_columns(ids, 0, N1, turned, halo_a, halo_b, state, weights, first, second)
    store = pltpu.make_async_copy(state, state_hbm, sems.at[2])
    store.start()
    emit, pack = row_packer(ids, out_a, out_b)

    def body(t, carry):
        pack(12 * t, lambda k: state[t, 8 * k : 8 * k + 8, :])
        return carry

    lax.fori_loop(0, N1, body, 0)
    keep = jnp.logical_or(iota((8, 128), 0) < 7, ids[0] < 7)
    for c in copies:
        c.wait()
    pack(WIND, lambda k: jnp.where(keep, merid[k], 0.0))
    emit(WIND + 12, surface[...], surface[...])
    emit(WIND + 13, left, left)
    emit(WIND + 14, right, right)
    store.wait()


def lon_second_kernel(ids, turned, halo_a, halo_b, weights, state_hbm, out_a, out_b, first, second, state, sems):
    sweep_columns(ids, N1, N2, turned, halo_a, halo_b, state, weights, first, second)
    store = pltpu.make_async_copy(state, state_hbm, sems.at[0])
    store.start()
    _, pack = row_packer(ids, out_a, out_b)

    def body(t, carry):
        pack(12 * t, lambda k: state[t, 8 * k : 8 * k + 8, :])
        return carry

    lax.fori_loop(0, N2, body, 0)
    store.wait()


def row_reader(ids, halo_a, halo_b):
    odd_lat = (ids[0] & 1) == 1
    sub = iota((8, 128), 0)

    def message(n):
        a, b = halo_a[n], halo_b[n]
        return jnp.where(odd_lat, a, b), jnp.where(odd_lat, b, a)

    def four(n):
        got = [message(n + x) for x in range(3)]
        rolled = [[pltpu.roll(got[x][y], 2 + 2 * x, 0) for x in range(3)] for y in range(2)]
        low = jnp.where(sub < 4, rolled[0][0], jnp.where(sub < 6, rolled[0][1], rolled[0][2]))
        high = jnp.where(sub < 2, rolled[1][0], jnp.where(sub < 4, rolled[1][1], rolled[1][2]))
        return got + [(low, high)]

    return message, four


def sweep_rows(count, four, latw, wide, swept):
    def unpack(t, carry):
        for g in range(4):
            for x, (low, high) in enumerate(four(12 * t + 3 * g)):
                k = 4 * g + x
                wide[t, k, 0:8], wide[t, k, 16:24] = low, high
        return carry

    lax.fori_loop(0, count, unpack, 0, unroll=2)

    def level(k, carry):
        v = [latw[k, m] for m in range(13)]
        for t in range(count):
            q = v[0] * wide[t, k, 2:10]
            for m in range(1, 13):
                q = q + v[m] * wide[t, k, 2 + m : 10 + m]
            swept[t, pl.ds(pl.multiple_of(8 * k, 8), 8), :] = q
        return carry

    lax.fori_loop(0, 16, level, 0)


def mix(matrix, x):
    high = x.astype(BF16)
    low = (x - high.astype(F32)).astype(BF16)
    return (
        jnp.dot(matrix[0], high, preferred_element_type=F32)
        + jnp.dot(matrix[0], low, preferred_element_type=F32)
        + jnp.dot(matrix[1], high, preferred_element_type=F32)
    )


def parts(x):
    high = x.astype(BF16)
    return high, (x - high.astype(F32)).astype(BF16)


def rows_kernel(
    ids,
    state_hbm,
    merid_hbm,
    a_hbm,
    b_hbm,
    edge,
    mixing_hbm,
    grid_in,
    out_hbm,
    latw,
    matrix,
    emitted,
    swept,
    wide,
    wind,
    merid,
    halo_a,
    halo_b,
    mixing,
    lonw,
    grid,
    second,
    back,
    out,
    sems,
):
    copies = load(
        [(a_hbm, halo_a), (b_hbm, halo_b), (merid_hbm, merid), (mixing_hbm, mixing), (state_hbm, wide.at[:, :, pl.ds(8, 8), :])], sems
    )
    sub = iota((8, 128), 0)
    keep = jnp.logical_or(sub < 7, ids[0] < 7)
    hi = lax.Precision.HIGHEST
    i, j = iota((128, 128), 0), iota((128, 128), 1)
    spread = jnp.where((j & 7) == i, 1.0, 0.0)

    def level_zero(n):
        wind[n] = jnp.dot(wind[n], spread, precision=hi, preferred_element_type=F32)
        zonal_weights(wind.at[n], lonw.at[n])

    wind[1] = edge[...]
    level_zero(1)
    copies[3].wait()
    order = jnp.where(((i & 7) * 16 + (i >> 3)) == j, 1.0, 0.0)
    by_level = jnp.dot(order, mixing[...], precision=hi, preferred_element_type=F32)
    expand = jnp.where((iota((16, 128), 1) >> 3) == iota((16, 128), 0), 1.0, 0.0)
    whole = jnp.dot(by_level, expand, precision=hi, preferred_element_type=F32)
    whole = jnp.where((i & 7) == (j & 7), whole, 0.0)
    matrix[...] = whole
    for c in copies[:3] + copies[4:]:
        c.wait()
    message, four = row_reader(ids, halo_a, halo_b)
    for g in range(4):
        for x, (low, high) in enumerate(four(WIND + 3 * g)):
            k = 4 * g + x
            v = lat_weights(jnp.where(keep, merid[k], 0.0), low, high, sub)
            for m in range(13):
                latw[k, m] = v[m]
    centre, left, right = message(WIND + 12), message(WIND + 13), message(WIND + 14)
    for n in (0, 2):
        m = n // 2
        wind[n, 0:8], wind[n, 136:144] = left[m], right[m]
        wind[n, 8:136] = jnp.concatenate([centre[m]] * 16, 0).T
        level_zero(n)
    for n in range(3):
        grid[n] = grid_in[n]
        zonal_steps_unrolled(lonw.at[n], grid.at[n], second.at[n])
    for n in range(3):
        x = grid[n, 8:136].T
        for t in range(16):
            back[t, 8 * n : 8 * n + 8] = x[8 * t : 8 * t + 8]
    for t in range(16):
        e = latw[0, 0] * back[t, 2:10]
        for m in range(1, 13):
            e = e + latw[0, m] * back[t, 2 + m : 10 + m]
        emitted[t] = e
    sweep_rows(N1, four, latw, wide, swept)
    split = parts(whole)
    for t in range(N1):
        swept[t, 0:8] = swept[t, 0:8] + emitted[t]
        out[t] = mix(split, swept[t])
    store = pltpu.make_async_copy(out, out_hbm.at[pl.ds(0, N1)], sems.at[0])
    store.start()
    store.wait()


def last_kernel(ids, state_hbm, halo_a, halo_b, latw, matrix, emitted, _, out_hbm, swept, wide, out, sems):
    copies = load([(state_hbm, wide.at[:, :, pl.ds(8, 8), :])], sems)
    split = parts(matrix[...])
    copies[0].wait()
    _, four = row_reader(ids, halo_a, halo_b)
    sweep_rows(N2, four, latw, wide, swept)
    half = N2 // 2
    stores = []
    for n, (first, count) in enumerate(((0, half), (half, N2 - half))):
        for t in range(first, first + count):
            swept[t, 0:8] = swept[t, 0:8] + emitted[N1 + t]
            out[t] = mix(split, swept[t])
        stores.append(
            pltpu.make_async_copy(out.at[pl.ds(first, count)], out_hbm.at[pl.ds(N1 + first, count)], sems.at[1 + n])
        )
        stores[-1].start()
    for c in stores:
        c.wait()


def scatter_kernel(got, grid, turned):
    sub = iota((8, 128), 0)
    spots = got[pl.ds(9, 128, stride=ROWS), :].T.astype(jnp.int32)
    row_of, col_of = spots >> 7, spots & 127

    def split(b):
        x = got[pl.ds(b, 128, stride=ROWS), :].T
        high = x.astype(BF16).astype(F32)
        return high, x - high

    def main(b):
        high, low = split(b)
        turned[0], turned[1] = high, low
        highs, lows, where = [], [], []
        target = iota((128, 128), 0)
        for s in range(8):
            here = row_of[8 * b + s : 8 * b + s + 1, :] == sub

            def rows(n):
                return jnp.concatenate(
                    [
                        jnp.where(here, jnp.broadcast_to(turned[n, 16 * s + t : 16 * s + t + 1, :], (8, 128)), 0.0)
                        for t in range(16)
                    ],
                    0,
                ).astype(BF16)

            highs.append(rows(0))
            lows.append(rows(1))
            where.append(jnp.where(col_of[8 * b + s : 8 * b + s + 1, :] == target, 1.0, 0.0).astype(BF16))
        where = jnp.concatenate(where, 1)
        return lax.dot_general(where, jnp.concatenate(highs, 1), NT, preferred_element_type=F32) + lax.dot_general(
            where, jnp.concatenate(lows, 1), NT, preferred_element_type=F32
        )

    expand = jnp.where((iota((32, 128), 0) & 15) == (iota((32, 128), 1) >> 3), 1.0, 0.0)
    diagonal = (iota((64, 128), 0) & 7) == (iota((64, 128), 1) & 7)

    def side(b, first):
        high, low = split(b)
        flux = jnp.concatenate(
            [jnp.concatenate([high[16 * s : 16 * s + 16], low[16 * s : 16 * s + 16]], 0) for s in range(8)], 1
        ).astype(BF16)
        key = (col_of - first) * 8 + row_of
        target = iota((64, 128), 0)
        where = jnp.concatenate(
            [jnp.where(key[8 * b + s : 8 * b + s + 1, :] == target, 1.0, 0.0) for s in range(8)], 1
        ).astype(BF16)
        sums = lax.dot_general(where, flux, NT, preferred_element_type=F32)
        sums = jnp.dot(sums, expand, precision=lax.Precision.HIGHEST, preferred_element_type=F32)
        sums = jnp.where(diagonal, sums, 0.0)
        return jnp.concatenate([jnp.sum(sums[8 * c : 8 * c + 8], 0, keepdims=True) for c in range(8)], 0)

    for n in range(3):
        grid[n, 0:8] = side(3 * n, 120)
        grid[n, 8:136] = main(3 * n + 1)
        grid[n, 136:144] = side(3 * n + 2, 0)


def call(kernel, ins, outs, scratch=(), kinds=None, copies=0, in_hbm=(), aliases=None, us=2):
    spec = {"s": pltpu.SMEM, "v": VM, "h": pltpu.HBM}
    rooms = [VM(x, F32) if isinstance(x, tuple) else x for x in scratch]
    if copies:
        rooms.append(pltpu.SemaphoreType.DMA((copies,)))
    return pl.pallas_call(
        kernel,
        out_shape=[pltpu.HBM(s, F32) if n in in_hbm else jax.ShapeDtypeStruct(s, F32) for n, s in enumerate(outs)],
        in_specs=[pl.BlockSpec(memory_space=spec[x]) for x in kinds],
        out_specs=[pl.BlockSpec(memory_space=pltpu.HBM if n in in_hbm else VM) for n in range(len(outs))],
        scratch_shapes=rooms,
        compiler_params=PARAMS,
        cost_estimate=pl.CostEstimate(flops=0, bytes_accessed=int(us * 3.6e6), transcendentals=0),
        input_output_aliases=aliases or {},
    )(*[pltpu.with_memory_space_constraint(x, pltpu.HBM) if k == "h" else x for x, k in zip(ins, kinds)])


def load(pairs, sems):
    copies = [pltpu.make_async_copy(x, y, sems.at[n]) for n, (x, y) in enumerate(pairs)]
    for c in copies:
        c.start()
    return copies


def on_device(
    features, land_tile, land_spot, w_in, b_in, w_mid, b_mid, w_out, tracers, zonal_wind, meridional_wind, mixing
):
    ids = jnp.stack([lax.axis_index("lat"), lax.axis_index("lon")]).astype(jnp.int32)
    shape = tracers.shape
    tracers = tracers.reshape(16, 128, 128)
    zonal = zonal_wind.reshape(128, 128)
    pack_a, pack_b, turned = call(
        pack_kernel,
        (ids, tracers, zonal),
        [(17, 8, 128), (17, 8, 128), (17, 128, 128)],
        scratch=[(16, 128, 128), (128, 128)],
        us=2,
        kinds="shh",
        copies=5,
    )
    lon_a = [(i, i ^ 1) for i in range(16)]
    lon_b = [(i, (i + 1) % 16 if i & 1 else (i - 1) % 16) for i in range(16)]
    lat_a = [(i, i ^ 1) for i in range(8)]
    lat_b = [(i, i + 1 if i & 1 else i - 1) for i in range(1, 7)]
    halo_b = lax.ppermute(pack_b, "lon", lon_b)
    halo_a = lax.ppermute(pack_a, "lon", lon_a)
    cells = features.shape[0]
    inputs = (
        features.T,
        land_tile.reshape(1, cells),
        land_spot.reshape(1, cells),
        w_in,
        b_in.reshape(1, -1),
        w_mid,
        b_mid.reshape(1, -1),
        w_out.T,
    )
    (message,) = call(
        flux_kernel,
        inputs,
        [(128 * ROWS, 128)],
        scratch=[VM(x.shape, x.dtype) for x in inputs],
        us=3,
        kinds="h" * 8,
        copies=8,
    )
    halo_a, halo_b, message = lax.optimization_barrier((halo_a, halo_b, message))
    state_one, one_a, one_b, edge, weights = call(
        lon_first_kernel,
        (ids, turned, zonal, meridional_wind, halo_a, halo_b),
        [(N1, 128, 128), (MSG1, 8, 128), (MSG1, 8, 128), (144, 128), (7, 136, 128)],
        scratch=[(N1, 144, 128), (N1, 136, 128), (16, 8, 128), (8, 128), (N1, 128, 128)],
        us=3,
        kinds="svhhvv",
        copies=3,
        in_hbm=(0,),
    )
    ones_a = lax.ppermute(one_a, "lat", lat_a)
    ones_b = lax.ppermute(one_b, "lat", lat_b)
    got = lax.all_to_all(
        message.reshape(128, 1, ROWS * 128), ("lat", "lon"), split_axis=0, concat_axis=0, tiled=True
    ).reshape(128 * ROWS, 128)
    state_two, two_a, two_b = call(
        lon_second_kernel,
        (ids, turned, halo_a, halo_b, weights),
        [(N2, 128, 128), (MSG2, 8, 128), (MSG2, 8, 128)],
        scratch=[(N2, 144, 128), (N2, 136, 128), (N2, 128, 128)],
        us=3,
        kinds="svvvv",
        copies=1,
        in_hbm=(0,),
    )
    twos_a = lax.ppermute(two_a, "lat", lat_a)
    twos_b = lax.ppermute(two_b, "lat", lat_b)
    (grid,) = call(scatter_kernel, (got,), [(3, 144, 128)], scratch=[(2, 128, 128)], kinds="v")
    ones_a, ones_b, grid = lax.optimization_barrier((ones_a, ones_b, grid))
    out, latw, matrix, emitted = call(
        rows_kernel,
        (ids, state_one.reshape(N1, 16, 8, 128), meridional_wind, ones_a, ones_b, edge, mixing.reshape(128, 16), grid),
        [(16, 128, 128), (16, 13, 8, 128), (128, 128), (16, 8, 128)],
        scratch=[
            (N1, 128, 128),
            (N1, 16, 24, 128),
            (3, 144, 128),
            (16, 8, 128),
            (MSG1, 8, 128),
            (MSG1, 8, 128),
            (128, 16),
            (3, 7, 136, 128),
            (3, 144, 128),
            (3, 136, 128),
            (16, 24, 128),
            (N1, 128, 128),
        ],
        us=5,
        kinds="shhhhvhv",
        copies=5,
        in_hbm=(0,),
    )
    (out,) = call(
        last_kernel,
        (ids, state_two.reshape(N2, 16, 8, 128), twos_a, twos_b, latw, matrix, emitted, out),
        [(16, 128, 128)],
        scratch=[
            (N2, 128, 128),
            (N2, 16, 24, 128),
            (N2, 128, 128),
        ],
        us=4,
        kinds="shvvvvvh",
        copies=3,
        in_hbm=(0,),
        aliases={7: 0},
    )
    return out.reshape(shape)


def solution(mesh):
    placed = (
        P(("lat", "lon"), None),
        P(("lat", "lon"), None),
        P(("lat", "lon")),
        P(),
        P(),
        P(),
        P(),
        P(),
        P(None, None, "lat", "lon"),
        P(None, "lat", "lon"),
        P(None, "lat", "lon"),
        P("lat", None, None),
    )
    return jax.shard_map(
        on_device,
        mesh=mesh,
        in_specs=placed,
        out_specs=P(None, None, "lat", "lon"),
        check_vma=False,
    )
```

```python
import jax
import jax.numpy as jnp
from jax import lax
from jax.experimental import pallas as pl
from jax.experimental.pallas import tpu as pltpu
from jax.sharding import PartitionSpec as P

F32 = jnp.float32
BF16 = jnp.bfloat16
NT = (((1,), (1,)), ((), ()))
TN = (((0,), (0,)), ((), ()))
ROWS = 10
N1 = 8
N2 = 16 - N1
WIND = 12 * N1
MSG1 = WIND + 15
MSG2 = 12 * N2
VM = pltpu.VMEM
PARAMS = pltpu.CompilerParams(vmem_limit_bytes=12 * 1024 * 1024)


def vspec():
    return pl.BlockSpec(memory_space=VM)


def iota(shape, dim):
    return lax.broadcasted_iota(jnp.int32, shape, dim)


def face_weights(c):
    pos = c >= 0
    w = jnp.abs(c)
    al = 0.5 * w * w
    be = 3.0 * al - 2.0 * al * w
    p = w - al - be
    g = al - be
    h = 2.0 * be
    p = jnp.where(pos, p, -p)
    zero = jnp.zeros_like(c)
    gp = jnp.where(pos, g, zero)
    gm = jnp.where(pos, zero, -g)
    hp = jnp.where(pos, h, zero)
    hm = jnp.where(pos, zero, -h)
    a, b = 7.0 / 12.0, 1.0 / 12.0
    return [
        -b * gp,
        a * gp - b * p,
        a * (p + gp) - b * gm + hp,
        a * (p + gm) - b * gp + hm,
        a * gm - b * p,
        -b * gm,
    ]


def step_weights(f, f_before):
    out = []
    for m in range(-3, 4):
        v = None
        if m <= 2:
            v = f_before[m + 3]
        if m >= -2:
            v = -f[m + 2] if v is None else v - f[m + 2]
        if m == 0:
            v = v + 1.0
        out.append(v)
    return out


def shifted(q, low, high, s, axis, pos):
    n = q.shape[axis]
    if s == 0:
        return q
    if s > 0:
        return pltpu.roll(jnp.where(pos < s, high, q), n - s, axis)
    return pltpu.roll(jnp.where(pos >= n + s, low, q), -s, axis)


def double_weights(w, w_low, w_high, axis, pos):
    out = [None] * 13
    for a in range(-3, 4):
        for b in range(-3, 4):
            v = w[a + 3] * shifted(w[b + 3], w_low[b + 3], w_high[b + 3], a, axis, pos)
            out[a + b + 6] = v if out[a + b + 6] is None else out[a + b + 6] + v
    return out


def zonal_weights(wind, out):
    for b in range(17):
        f = face_weights(wind[8 * b + 5 : 8 * b + 13])
        before = face_weights(wind[8 * b + 4 : 8 * b + 12])
        for m, w in enumerate(step_weights(f, before)):
            out[m, 8 * b : 8 * b + 8] = w


def zonal_steps_unrolled(weights, first, second):
    def total(terms):
        while len(terms) > 1:
            terms = [x + y for x, y in zip(terms[::2], terms[1::2])] + ([terms[-1]] if len(terms) & 1 else [])
        return terms[0]

    for b in range(17):
        second[8 * b : 8 * b + 8] = total(
            [weights[m, 8 * b : 8 * b + 8, :] * first[8 * b + 2 + m : 8 * b + 10 + m] for m in range(7)]
        )
    for b in range(16):
        first[8 * b + 8 : 8 * b + 16] = total(
            [weights[m, 8 * b + 3 : 8 * b + 11, :] * second[8 * b + m : 8 * b + 8 + m] for m in range(7)]
        )


def zonal_steps(weights, first, second, count):
    def one(b, carry):
        w = [weights[m, pl.ds(pl.multiple_of(8 * b, 8), 8), :] for m in range(7)]
        for t in range(count):
            v = w[0] * first[t, pl.ds(8 * b + 2, 8), :]
            for m in range(1, 7):
                v = v + w[m] * first[t, pl.ds(8 * b + 2 + m, 8), :]
            second[t, pl.ds(pl.multiple_of(8 * b, 8), 8), :] = v
        return carry

    lax.fori_loop(0, 17, one, 0)

    def two(b, carry):
        w = [weights[m, pl.ds(8 * b + 3, 8), :] for m in range(7)]
        for t in range(count):
            v = w[0] * second[t, pl.ds(8 * b, 8), :]
            for m in range(1, 7):
                v = v + w[m] * second[t, pl.ds(8 * b + m, 8), :]
            first[t, pl.ds(pl.multiple_of(8 * b + 8, 8), 8), :] = v
        return carry

    lax.fori_loop(0, 16, two, 0)


def lat_weights(c, low, high, sub):
    f, fl, fh = face_weights(c), face_weights(low), face_weights(high)
    before = [shifted(x, y, y, -1, 0, sub) for x, y in zip(f, fl)]
    low_before = [shifted(y, y, y, -1, 0, sub) for y in fl]
    high_before = [shifted(y, x, x, -1, 0, sub) for x, y in zip(f, fh)]
    w = step_weights(f, before)
    wl = step_weights(fl, low_before)
    wh = step_weights(fh, high_before)
    return double_weights(w, wl, wh, 0, sub)


def pack_kernel(ids, tracers_hbm, zonal_hbm, *refs):
    flux_in, (out_a, out_b, turned), flux_out, (tracers, zonal, sems) = refs[:8], refs[8:11], refs[11:19], refs[19:]
    odd = (ids[1] & 1) == 1
    chunks = [(zonal_hbm, zonal)]
    chunks += [(tracers_hbm.at[pl.ds(4 * n, 4)], tracers.at[pl.ds(4 * n, 4)]) for n in range(4)]
    copies = load(chunks + list(zip(flux_in, flux_out)), sems)

    def put(t, x):
        x = x.T
        turned[t] = x
        left, right = x[0:8], x[120:128]
        out_a[t] = jnp.where(odd, left, right)
        out_b[t] = jnp.where(odd, right, left)

    copies[0].wait()
    put(16, zonal[...])
    for n in range(4):
        copies[n + 1].wait()
        for t in range(4 * n, 4 * n + 4):
            put(t, tracers[t])
    for c in copies[5:]:
        c.wait()


def flux_kernel(feat, tile, spot, w_in, b_in, w_mid, b_mid, w_out, out):
    def silu(v):
        return (v / (1.0 + jnp.exp(-v))).astype(BF16)

    first = silu(lax.dot_general(feat[...], w_in[...], TN, preferred_element_type=F32) + b_in[...])
    second = silu(jnp.dot(first, w_mid[...], preferred_element_type=F32) + b_mid[...])
    flux = lax.dot_general(w_out[...], second, NT, preferred_element_type=F32)
    cells = flux.shape[1]
    member = iota((128, cells), 0) == tile[...]
    member32 = jnp.where(member, 1.0, 0.0)
    member16 = member32.astype(BF16)
    upper = jnp.where(iota((cells, cells), 0) < iota((cells, cells), 1), 1.0, 0.0).astype(BF16)
    earlier = jnp.dot(member16, upper, preferred_element_type=F32)
    slot = jnp.sum(member32 * earlier, axis=0, keepdims=True).astype(jnp.int32)
    high = flux.astype(BF16).astype(F32)
    low = flux - high
    zero = jnp.zeros_like(flux)
    rows_high = jnp.concatenate([jnp.where(slot == s, high, zero) for s in range(8)], 0)
    rows_low = jnp.concatenate([jnp.where(slot == s, low, zero) for s in range(8)], 0)
    sent = lax.dot_general(
        member16, rows_high.astype(BF16), NT, preferred_element_type=F32
    ) + lax.dot_general(member16, rows_low.astype(BF16), NT, preferred_element_type=F32)
    here = (iota((128, cells), 0) & 7) == slot
    places = spot[...]
    coarse = jnp.where(here, (places >> 4) << 4, 0).astype(F32).astype(BF16)
    fine = jnp.where(here, places & 15, 0).astype(F32).astype(BF16)
    spots = lax.dot_general(member16, coarse, NT, preferred_element_type=F32) + lax.dot_general(
        member16, fine, NT, preferred_element_type=F32
    )
    row = iota((128, 128), 0)
    group = iota((128, 128), 1) >> 3

    def beside(x, dn):
        if dn == 0:
            return x
        if dn == 1:
            return jnp.where((row & 15) == 15, pltpu.roll(x, 15, 0), pltpu.roll(x, 127, 0))
        return jnp.where((row & 15) == 0, pltpu.roll(x, 113, 0), pltpu.roll(x, 1, 0))

    def above(x, dl):
        pad = jnp.zeros((16, 128), F32)
        if dl == 0:
            return x
        if dl == 1:
            return jnp.concatenate([x[16:], pad], 0)
        return jnp.concatenate([pad, x[:-16]], 0)

    places_out = jnp.zeros((128, 128), F32)
    for dn in (-1, 0, 1):
        x, y = beside(sent, dn), beside(spots, dn)
        for dl in (-1, 0, 1):
            b = (dl + 1) * 3 + dn + 1
            out[pl.ds(b, 128, stride=ROWS), :] = above(x, dl)
            places_out = jnp.where(group == b, above(y, dl), places_out)
    out[pl.ds(9, 128, stride=ROWS), :] = places_out


def sweep_columns(ids, base, count, turned, halo_a, halo_b, state, weights, first, second):
    odd = (ids[1] & 1) == 1
    for t in range(count):
        a, b = halo_a[base + t], halo_b[base + t]
        first[t, 0:8], first[t, 136:144] = jnp.where(odd, a, b), jnp.where(odd, b, a)
        first[t, 8:136] = turned[base + t]
    zonal_steps(weights, first, second, count)
    for t in range(count):
        state[t] = first[t, 8:136].T


def row_packer(ids, out_a, out_b):
    odd_lat = (ids[0] & 1) == 1
    sub = iota((8, 128), 0)

    def emit(n, up, down):
        out_a[n] = jnp.where(odd_lat, down, up)
        out_b[n] = jnp.where(odd_lat, up, down)

    def pack(n, read):
        for g in range(4):
            q = [read(4 * g + i) for i in range(4)]
            for i in range(3):
                last = pltpu.roll(q[3], 6 - 2 * i, 0)
                emit(n + g * 3 + i, jnp.where(sub >= 2, q[i], last), jnp.where(sub < 6, q[i], last))

    return emit, pack


def lon_first_kernel(
    ids, turned, zonal, merid_hbm, halo_a, halo_b, state_hbm, out_a, out_b, wind, weights, first, second, merid, surface, state, sems
):
    copies = load([(merid_hbm, merid), (zonal.at[pl.ds(0, 8)], surface)], sems)
    odd = (ids[1] & 1) == 1
    a, b = halo_a[16], halo_b[16]
    left, right = jnp.where(odd, a, b), jnp.where(odd, b, a)
    wind[0:8], wind[8:136], wind[136:144] = left, turned[16], right
    zonal_weights(wind, weights)
    sweep_columns(ids, 0, N1, turned, halo_a, halo_b, state, weights, first, second)
    store = pltpu.make_async_copy(state, state_hbm, sems.at[2])
    store.start()
    emit, pack = row_packer(ids, out_a, out_b)

    def body(t, carry):
        pack(12 * t, lambda k: state[t, 8 * k : 8 * k + 8, :])
        return carry

    lax.fori_loop(0, N1, body, 0)
    keep = jnp.logical_or(iota((8, 128), 0) < 7, ids[0] < 7)
    for c in copies:
        c.wait()
    pack(WIND, lambda k: jnp.where(keep, merid[k], 0.0))
    emit(WIND + 12, surface[...], surface[...])
    emit(WIND + 13, left, left)
    emit(WIND + 14, right, right)
    store.wait()


def lon_second_kernel(ids, turned, halo_a, halo_b, weights, state_hbm, out_a, out_b, first, second, state, sems):
    sweep_columns(ids, N1, N2, turned, halo_a, halo_b, state, weights, first, second)
    store = pltpu.make_async_copy(state, state_hbm, sems.at[0])
    store.start()
    _, pack = row_packer(ids, out_a, out_b)

    def body(t, carry):
        pack(12 * t, lambda k: state[t, 8 * k : 8 * k + 8, :])
        return carry

    lax.fori_loop(0, N2, body, 0)
    store.wait()


def row_reader(ids, halo_a, halo_b):
    odd_lat = (ids[0] & 1) == 1
    sub = iota((8, 128), 0)

    def message(n):
        a, b = halo_a[n], halo_b[n]
        return jnp.where(odd_lat, a, b), jnp.where(odd_lat, b, a)

    def four(n):
        got = [message(n + x) for x in range(3)]
        rolled = [[pltpu.roll(got[x][y], 2 + 2 * x, 0) for x in range(3)] for y in range(2)]
        low = jnp.where(sub < 4, rolled[0][0], jnp.where(sub < 6, rolled[0][1], rolled[0][2]))
        high = jnp.where(sub < 2, rolled[1][0], jnp.where(sub < 4, rolled[1][1], rolled[1][2]))
        return got + [(low, high)]

    return message, four


def sweep_rows(count, four, latw, wide, swept):
    def unpack(t, carry):
        for g in range(4):
            for x, (low, high) in enumerate(four(12 * t + 3 * g)):
                k = 4 * g + x
                wide[t, k, 0:8], wide[t, k, 16:24] = low, high
        return carry

    lax.fori_loop(0, count, unpack, 0, unroll=2)

    def level(k, carry):
        v = [latw[k, m] for m in range(13)]
        for t in range(count):
            q = v[0] * wide[t, k, 2:10]
            for m in range(1, 13):
                q = q + v[m] * wide[t, k, 2 + m : 10 + m]
            swept[t, pl.ds(pl.multiple_of(8 * k, 8), 8), :] = q
        return carry

    lax.fori_loop(0, 16, level, 0)


def mix(matrix, x):
    high = x.astype(BF16)
    low = (x - high.astype(F32)).astype(BF16)
    return (
        jnp.dot(matrix[0], high, preferred_element_type=F32)
        + jnp.dot(matrix[0], low, preferred_element_type=F32)
        + jnp.dot(matrix[1], high, preferred_element_type=F32)
    )


def parts(x):
    high = x.astype(BF16)
    return high, (x - high.astype(F32)).astype(BF16)


def rows_kernel(
    ids,
    state_hbm,
    merid_hbm,
    a_hbm,
    b_hbm,
    edge,
    mixing_hbm,
    grid_in,
    two_hbm,
    out_hbm,
    latw,
    matrix,
    emitted,
    two,
    swept,
    wide,
    wind,
    merid,
    halo_a,
    halo_b,
    mixing,
    lonw,
    grid,
    second,
    back,
    out,
    sems,
):
    copies = load(
        [(a_hbm, halo_a), (b_hbm, halo_b), (merid_hbm, merid), (mixing_hbm, mixing), (state_hbm, wide.at[:, :, pl.ds(8, 8), :])], sems
    )
    fetch = pltpu.make_async_copy(two_hbm, two, sems.at[5])
    fetch.start()
    sub = iota((8, 128), 0)
    keep = jnp.logical_or(sub < 7, ids[0] < 7)
    hi = lax.Precision.HIGHEST
    i, j = iota((128, 128), 0), iota((128, 128), 1)
    spread = jnp.where((j & 7) == i, 1.0, 0.0)

    def level_zero(n):
        wind[n] = jnp.dot(wind[n], spread, precision=hi, preferred_element_type=F32)
        zonal_weights(wind.at[n], lonw.at[n])

    wind[1] = edge[...]
    level_zero(1)
    copies[3].wait()
    order = jnp.where(((i & 7) * 16 + (i >> 3)) == j, 1.0, 0.0)
    by_level = jnp.dot(order, mixing[...], precision=hi, preferred_element_type=F32)
    expand = jnp.where((iota((16, 128), 1) >> 3) == iota((16, 128), 0), 1.0, 0.0)
    whole = jnp.dot(by_level, expand, precision=hi, preferred_element_type=F32)
    whole = jnp.where((i & 7) == (j & 7), whole, 0.0)
    matrix[...] = whole
    for c in copies[:3] + copies[4:]:
        c.wait()
    message, four = row_reader(ids, halo_a, halo_b)
    for g in range(4):
        for x, (low, high) in enumerate(four(WIND + 3 * g)):
            k = 4 * g + x
            v = lat_weights(jnp.where(keep, merid[k], 0.0), low, high, sub)
            for m in range(13):
                latw[k, m] = v[m]
    centre, left, right = message(WIND + 12), message(WIND + 13), message(WIND + 14)
    for n in (0, 2):
        m = n // 2
        wind[n, 0:8], wind[n, 136:144] = left[m], right[m]
        wind[n, 8:136] = jnp.concatenate([centre[m]] * 16, 0).T
        level_zero(n)
    for n in range(3):
        grid[n] = grid_in[n]
        zonal_steps_unrolled(lonw.at[n], grid.at[n], second.at[n])
    for n in range(3):
        x = grid[n, 8:136].T
        for t in range(16):
            back[t, 8 * n : 8 * n + 8] = x[8 * t : 8 * t + 8]
    for t in range(16):
        e = latw[0, 0] * back[t, 2:10]
        for m in range(1, 13):
            e = e + latw[0, m] * back[t, 2 + m : 10 + m]
        emitted[t] = e
    sweep_rows(N1, four, latw, wide, swept)
    split = parts(whole)
    for t in range(N1):
        swept[t, 0:8] = swept[t, 0:8] + emitted[t]
        out[t] = mix(split, swept[t])
    store = pltpu.make_async_copy(out, out_hbm.at[pl.ds(0, N1)], sems.at[0])
    store.start()
    fetch.wait()
    store.wait()


def last_kernel(ids, state, halo_a, halo_b, latw, matrix, emitted, _, out_hbm, swept, wide, out, sems):
    split = parts(matrix[...])
    for t in range(N2):
        for k in range(16):
            wide[t, k, 8:16] = state[t, 8 * k : 8 * k + 8]
    _, four = row_reader(ids, halo_a, halo_b)
    sweep_rows(N2, four, latw, wide, swept)
    half = N2 // 2
    stores = []
    for n, (first, count) in enumerate(((0, half), (half, N2 - half))):
        for t in range(first, first + count):
            swept[t, 0:8] = swept[t, 0:8] + emitted[N1 + t]
            out[t] = mix(split, swept[t])
        stores.append(
            pltpu.make_async_copy(out.at[pl.ds(first, count)], out_hbm.at[pl.ds(N1 + first, count)], sems.at[1 + n])
        )
        stores[-1].start()
    for c in stores:
        c.wait()


def scatter_kernel(got, grid, turned):
    sub = iota((8, 128), 0)
    spots = got[pl.ds(9, 128, stride=ROWS), :].T.astype(jnp.int32)
    row_of, col_of = spots >> 7, spots & 127

    def split(b):
        x = got[pl.ds(b, 128, stride=ROWS), :].T
        high = x.astype(BF16).astype(F32)
        return high, x - high

    def main(b):
        high, low = split(b)
        turned[0], turned[1] = high, low
        highs, lows, where = [], [], []
        target = iota((128, 128), 0)
        for s in range(8):
            here = row_of[8 * b + s : 8 * b + s + 1, :] == sub

            def rows(n):
                return jnp.concatenate(
                    [
                        jnp.where(here, jnp.broadcast_to(turned[n, 16 * s + t : 16 * s + t + 1, :], (8, 128)), 0.0)
                        for t in range(16)
                    ],
                    0,
                ).astype(BF16)

            highs.append(rows(0))
            lows.append(rows(1))
            where.append(jnp.where(col_of[8 * b + s : 8 * b + s + 1, :] == target, 1.0, 0.0).astype(BF16))
        where = jnp.concatenate(where, 1)
        return lax.dot_general(where, jnp.concatenate(highs, 1), NT, preferred_element_type=F32) + lax.dot_general(
            where, jnp.concatenate(lows, 1), NT, preferred_element_type=F32
        )

    expand = jnp.where((iota((32, 128), 0) & 15) == (iota((32, 128), 1) >> 3), 1.0, 0.0)
    diagonal = (iota((64, 128), 0) & 7) == (iota((64, 128), 1) & 7)

    def side(b, first):
        high, low = split(b)
        flux = jnp.concatenate(
            [jnp.concatenate([high[16 * s : 16 * s + 16], low[16 * s : 16 * s + 16]], 0) for s in range(8)], 1
        ).astype(BF16)
        key = (col_of - first) * 8 + row_of
        target = iota((64, 128), 0)
        where = jnp.concatenate(
            [jnp.where(key[8 * b + s : 8 * b + s + 1, :] == target, 1.0, 0.0) for s in range(8)], 1
        ).astype(BF16)
        sums = lax.dot_general(where, flux, NT, preferred_element_type=F32)
        sums = jnp.dot(sums, expand, precision=lax.Precision.HIGHEST, preferred_element_type=F32)
        sums = jnp.where(diagonal, sums, 0.0)
        return jnp.concatenate([jnp.sum(sums[8 * c : 8 * c + 8], 0, keepdims=True) for c in range(8)], 0)

    for n in range(3):
        grid[n, 0:8] = side(3 * n, 120)
        grid[n, 8:136] = main(3 * n + 1)
        grid[n, 136:144] = side(3 * n + 2, 0)


def call(kernel, ins, outs, scratch=(), kinds=None, copies=0, in_hbm=(), aliases=None, us=2):
    spec = {"s": pltpu.SMEM, "v": VM, "h": pltpu.HBM}
    rooms = [VM(x, F32) if isinstance(x, tuple) else x for x in scratch]
    if copies:
        rooms.append(pltpu.SemaphoreType.DMA((copies,)))
    return pl.pallas_call(
        kernel,
        out_shape=[pltpu.HBM(s, F32) if n in in_hbm else struct(s) for n, s in enumerate(outs)],
        in_specs=[pl.BlockSpec(memory_space=spec[x]) for x in kinds],
        out_specs=[pl.BlockSpec(memory_space=pltpu.HBM if n in in_hbm else VM) for n in range(len(outs))],
        scratch_shapes=rooms,
        compiler_params=PARAMS,
        cost_estimate=pl.CostEstimate(flops=0, bytes_accessed=int(us * 3.6e6), transcendentals=0),
        input_output_aliases=aliases or {},
    )(*[pltpu.with_memory_space_constraint(x, pltpu.HBM) if k == "h" else x for x, k in zip(ins, kinds)])


def struct(s):
    return jax.ShapeDtypeStruct(s, F32) if isinstance(s, tuple) else jax.ShapeDtypeStruct(s.shape, s.dtype)


def load(pairs, sems):
    copies = [pltpu.make_async_copy(x, y, sems.at[n]) for n, (x, y) in enumerate(pairs)]
    for c in copies:
        c.start()
    return copies


def on_device(
    features, land_tile, land_spot, w_in, b_in, w_mid, b_mid, w_out, tracers, zonal_wind, meridional_wind, mixing
):
    ids = jnp.stack([lax.axis_index("lat"), lax.axis_index("lon")]).astype(jnp.int32)
    shape = tracers.shape
    tracers = tracers.reshape(16, 128, 128)
    zonal = zonal_wind.reshape(128, 128)
    cells = features.shape[0]
    inputs = (
        features.T,
        land_tile.reshape(1, cells),
        land_spot.reshape(1, cells),
        w_in,
        b_in.reshape(1, -1),
        w_mid,
        b_mid.reshape(1, -1),
        w_out.T,
    )
    pack_a, pack_b, turned, *inputs = call(
        pack_kernel,
        (ids, tracers, zonal) + inputs,
        [(17, 8, 128), (17, 8, 128), (17, 128, 128)] + list(inputs),
        scratch=[(16, 128, 128), (128, 128)],
        us=2,
        kinds="shh" + "h" * 8,
        copies=13,
    )
    lon_a = [(i, i ^ 1) for i in range(16)]
    lon_b = [(i, (i + 1) % 16 if i & 1 else (i - 1) % 16) for i in range(16)]
    lat_a = [(i, i ^ 1) for i in range(8)]
    lat_b = [(i, i + 1 if i & 1 else i - 1) for i in range(1, 7)]
    halo_b = lax.ppermute(pack_b, "lon", lon_b)
    halo_a = lax.ppermute(pack_a, "lon", lon_a)
    (message,) = call(flux_kernel, inputs, [(128 * ROWS, 128)], us=3, kinds="v" * 8)
    halo_a, halo_b, message = lax.optimization_barrier((halo_a, halo_b, message))
    state_one, one_a, one_b, edge, weights = call(
        lon_first_kernel,
        (ids, turned, zonal, meridional_wind, halo_a, halo_b),
        [(N1, 128, 128), (MSG1, 8, 128), (MSG1, 8, 128), (144, 128), (7, 136, 128)],
        scratch=[(N1, 144, 128), (N1, 136, 128), (16, 8, 128), (8, 128), (N1, 128, 128)],
        us=3,
        kinds="svhhvv",
        copies=3,
        in_hbm=(0,),
    )
    ones_a = lax.ppermute(one_a, "lat", lat_a)
    ones_b = lax.ppermute(one_b, "lat", lat_b)
    got = lax.all_to_all(
        message.reshape(128, 1, ROWS * 128), ("lat", "lon"), split_axis=0, concat_axis=0, tiled=True
    ).reshape(128 * ROWS, 128)
    state_two, two_a, two_b = call(
        lon_second_kernel,
        (ids, turned, halo_a, halo_b, weights),
        [(N2, 128, 128), (MSG2, 8, 128), (MSG2, 8, 128)],
        scratch=[(N2, 144, 128), (N2, 136, 128), (N2, 128, 128)],
        us=3,
        kinds="svvvv",
        copies=1,
        in_hbm=(0,),
    )
    twos_a = lax.ppermute(two_a, "lat", lat_a)
    twos_b = lax.ppermute(two_b, "lat", lat_b)
    (grid,) = call(scatter_kernel, (got,), [(3, 144, 128)], scratch=[(2, 128, 128)], kinds="v")
    ones_a, ones_b, grid = lax.optimization_barrier((ones_a, ones_b, grid))
    out, latw, matrix, emitted, state_two = call(
        rows_kernel,
        (ids, state_one.reshape(N1, 16, 8, 128), meridional_wind, ones_a, ones_b, edge, mixing.reshape(128, 16), grid, state_two),
        [(16, 128, 128), (16, 13, 8, 128), (128, 128), (16, 8, 128), (N2, 128, 128)],
        scratch=[
            (N1, 128, 128),
            (N1, 16, 24, 128),
            (3, 144, 128),
            (16, 8, 128),
            (MSG1, 8, 128),
            (MSG1, 8, 128),
            (128, 16),
            (3, 7, 136, 128),
            (3, 144, 128),
            (3, 136, 128),
            (16, 24, 128),
            (N1, 128, 128),
        ],
        us=5,
        kinds="shhhhvhvh",
        copies=6,
        in_hbm=(0,),
    )
    (out,) = call(
        last_kernel,
        (ids, state_two, twos_a, twos_b, latw, matrix, emitted, out),
        [(16, 128, 128)],
        scratch=[
            (N2, 128, 128),
            (N2, 16, 24, 128),
            (N2, 128, 128),
        ],
        us=4,
        kinds="svvvvvvh",
        copies=3,
        in_hbm=(0,),
        aliases={7: 0},
    )
    return out.reshape(shape)


def solution(mesh):
    placed = (
        P(("lat", "lon"), None),
        P(("lat", "lon"), None),
        P(("lat", "lon")),
        P(),
        P(),
        P(),
        P(),
        P(),
        P(None, None, "lat", "lon"),
        P(None, "lat", "lon"),
        P(None, "lat", "lon"),
        P("lat", None, None),
    )
    return jax.shard_map(
        on_device,
        mesh=mesh,
        in_specs=placed,
        out_specs=P(None, None, "lat", "lon"),
        check_vma=False,
    )
```

```python
import jax
import jax.numpy as jnp
from jax import lax
from jax.experimental import pallas as pl
from jax.experimental.pallas import tpu as pltpu
from jax.sharding import PartitionSpec as P

F32 = jnp.float32
BF16 = jnp.bfloat16
NT = (((1,), (1,)), ((), ()))
TN = (((0,), (0,)), ((), ()))
ROWS = 10
N1 = 9
N2 = 16 - N1
WIND = 12 * N1
MSG1 = WIND + 15
MSG2 = 12 * N2
VM = pltpu.VMEM
PARAMS = pltpu.CompilerParams(vmem_limit_bytes=12 * 1024 * 1024)


def vspec():
    return pl.BlockSpec(memory_space=VM)


def iota(shape, dim):
    return lax.broadcasted_iota(jnp.int32, shape, dim)


def face_weights(c):
    pos = c >= 0
    w = jnp.abs(c)
    al = 0.5 * w * w
    be = 3.0 * al - 2.0 * al * w
    p = w - al - be
    g = al - be
    h = 2.0 * be
    p = jnp.where(pos, p, -p)
    zero = jnp.zeros_like(c)
    gp = jnp.where(pos, g, zero)
    gm = jnp.where(pos, zero, -g)
    hp = jnp.where(pos, h, zero)
    hm = jnp.where(pos, zero, -h)
    a, b = 7.0 / 12.0, 1.0 / 12.0
    return [
        -b * gp,
        a * gp - b * p,
        a * (p + gp) - b * gm + hp,
        a * (p + gm) - b * gp + hm,
        a * gm - b * p,
        -b * gm,
    ]


def step_weights(f, f_before):
    out = []
    for m in range(-3, 4):
        v = None
        if m <= 2:
            v = f_before[m + 3]
        if m >= -2:
            v = -f[m + 2] if v is None else v - f[m + 2]
        if m == 0:
            v = v + 1.0
        out.append(v)
    return out


def shifted(q, low, high, s, axis, pos):
    n = q.shape[axis]
    if s == 0:
        return q
    if s > 0:
        return pltpu.roll(jnp.where(pos < s, high, q), n - s, axis)
    return pltpu.roll(jnp.where(pos >= n + s, low, q), -s, axis)


def double_weights(w, w_low, w_high, axis, pos):
    out = [None] * 13
    for a in range(-3, 4):
        for b in range(-3, 4):
            v = w[a + 3] * shifted(w[b + 3], w_low[b + 3], w_high[b + 3], a, axis, pos)
            out[a + b + 6] = v if out[a + b + 6] is None else out[a + b + 6] + v
    return out


def zonal_weights(wind, out):
    for b in range(17):
        f = face_weights(wind[8 * b + 5 : 8 * b + 13])
        before = face_weights(wind[8 * b + 4 : 8 * b + 12])
        for m, w in enumerate(step_weights(f, before)):
            out[m, 8 * b : 8 * b + 8] = w


def zonal_steps_unrolled(weights, first, second):
    def total(terms):
        while len(terms) > 1:
            terms = [x + y for x, y in zip(terms[::2], terms[1::2])] + ([terms[-1]] if len(terms) & 1 else [])
        return terms[0]

    for b in range(17):
        second[8 * b : 8 * b + 8] = total(
            [weights[m, 8 * b : 8 * b + 8, :] * first[8 * b + 2 + m : 8 * b + 10 + m] for m in range(7)]
        )
    for b in range(16):
        first[8 * b + 8 : 8 * b + 16] = total(
            [weights[m, 8 * b + 3 : 8 * b + 11, :] * second[8 * b + m : 8 * b + 8 + m] for m in range(7)]
        )


def zonal_steps(weights, first, second, count):
    def one(b, carry):
        w = [weights[m, pl.ds(pl.multiple_of(8 * b, 8), 8), :] for m in range(7)]
        for t in range(count):
            v = w[0] * first[t, pl.ds(8 * b + 2, 8), :]
            for m in range(1, 7):
                v = v + w[m] * first[t, pl.ds(8 * b + 2 + m, 8), :]
            second[t, pl.ds(pl.multiple_of(8 * b, 8), 8), :] = v
        return carry

    lax.fori_loop(0, 17, one, 0)

    def two(b, carry):
        w = [weights[m, pl.ds(8 * b + 3, 8), :] for m in range(7)]
        for t in range(count):
            v = w[0] * second[t, pl.ds(8 * b, 8), :]
            for m in range(1, 7):
                v = v + w[m] * second[t, pl.ds(8 * b + m, 8), :]
            first[t, pl.ds(pl.multiple_of(8 * b + 8, 8), 8), :] = v
        return carry

    lax.fori_loop(0, 16, two, 0)


def lat_weights(c, low, high, sub):
    f, fl, fh = face_weights(c), face_weights(low), face_weights(high)
    before = [shifted(x, y, y, -1, 0, sub) for x, y in zip(f, fl)]
    low_before = [shifted(y, y, y, -1, 0, sub) for y in fl]
    high_before = [shifted(y, x, x, -1, 0, sub) for x, y in zip(f, fh)]
    w = step_weights(f, before)
    wl = step_weights(fl, low_before)
    wh = step_weights(fh, high_before)
    return double_weights(w, wl, wh, 0, sub)


def pack_kernel(ids, tracers_hbm, zonal_hbm, *refs):
    flux_in, (out_a, out_b, turned), flux_out, (tracers, zonal, sems) = refs[:8], refs[8:11], refs[11:19], refs[19:]
    odd = (ids[1] & 1) == 1
    chunks = [(zonal_hbm, zonal)]
    chunks += [(tracers_hbm.at[pl.ds(4 * n, 4)], tracers.at[pl.ds(4 * n, 4)]) for n in range(4)]
    copies = load(chunks + list(zip(flux_in, flux_out)), sems)

    def put(t, x):
        x = x.T
        turned[t] = x
        left, right = x[0:8], x[120:128]
        out_a[t] = jnp.where(odd, left, right)
        out_b[t] = jnp.where(odd, right, left)

    copies[0].wait()
    put(16, zonal[...])
    for n in range(4):
        copies[n + 1].wait()
        for t in range(4 * n, 4 * n + 4):
            put(t, tracers[t])
    for c in copies[5:]:
        c.wait()


def flux_kernel(feat, tile, spot, w_in, b_in, w_mid, b_mid, w_out, out):
    def silu(v):
        return (v / (1.0 + jnp.exp(-v))).astype(BF16)

    first = silu(lax.dot_general(feat[...], w_in[...], TN, preferred_element_type=F32) + b_in[...])
    second = silu(jnp.dot(first, w_mid[...], preferred_element_type=F32) + b_mid[...])
    flux = lax.dot_general(w_out[...], second, NT, preferred_element_type=F32)
    cells = flux.shape[1]
    member = iota((128, cells), 0) == tile[...]
    member32 = jnp.where(member, 1.0, 0.0)
    member16 = member32.astype(BF16)
    upper = jnp.where(iota((cells, cells), 0) < iota((cells, cells), 1), 1.0, 0.0).astype(BF16)
    earlier = jnp.dot(member16, upper, preferred_element_type=F32)
    slot = jnp.sum(member32 * earlier, axis=0, keepdims=True).astype(jnp.int32)
    high = flux.astype(BF16).astype(F32)
    low = flux - high
    zero = jnp.zeros_like(flux)
    rows_high = jnp.concatenate([jnp.where(slot == s, high, zero) for s in range(8)], 0)
    rows_low = jnp.concatenate([jnp.where(slot == s, low, zero) for s in range(8)], 0)
    sent = lax.dot_general(
        member16, rows_high.astype(BF16), NT, preferred_element_type=F32
    ) + lax.dot_general(member16, rows_low.astype(BF16), NT, preferred_element_type=F32)
    here = (iota((128, cells), 0) & 7) == slot
    places = spot[...]
    coarse = jnp.where(here, (places >> 4) << 4, 0).astype(F32).astype(BF16)
    fine = jnp.where(here, places & 15, 0).astype(F32).astype(BF16)
    spots = lax.dot_general(member16, coarse, NT, preferred_element_type=F32) + lax.dot_general(
        member16, fine, NT, preferred_element_type=F32
    )
    row = iota((128, 128), 0)
    group = iota((128, 128), 1) >> 3

    def beside(x, dn):
        if dn == 0:
            return x
        if dn == 1:
            return jnp.where((row & 15) == 15, pltpu.roll(x, 15, 0), pltpu.roll(x, 127, 0))
        return jnp.where((row & 15) == 0, pltpu.roll(x, 113, 0), pltpu.roll(x, 1, 0))

    def above(x, dl):
        pad = jnp.zeros((16, 128), F32)
        if dl == 0:
            return x
        if dl == 1:
            return jnp.concatenate([x[16:], pad], 0)
        return jnp.concatenate([pad, x[:-16]], 0)

    places_out = jnp.zeros((128, 128), F32)
    for dn in (-1, 0, 1):
        x, y = beside(sent, dn), beside(spots, dn)
        for dl in (-1, 0, 1):
            b = (dl + 1) * 3 + dn + 1
            out[pl.ds(b, 128, stride=ROWS), :] = above(x, dl)
            places_out = jnp.where(group == b, above(y, dl), places_out)
    out[pl.ds(9, 128, stride=ROWS), :] = places_out


def sweep_columns(ids, base, count, turned, halo_a, halo_b, state, weights, first, second):
    odd = (ids[1] & 1) == 1
    for t in range(count):
        a, b = halo_a[base + t], halo_b[base + t]
        first[t, 0:8], first[t, 136:144] = jnp.where(odd, a, b), jnp.where(odd, b, a)
        first[t, 8:136] = turned[base + t]
    zonal_steps(weights, first, second, count)
    for t in range(count):
        state[t] = first[t, 8:136].T


def row_packer(ids, out_a, out_b):
    odd_lat = (ids[0] & 1) == 1
    sub = iota((8, 128), 0)

    def emit(n, up, down):
        out_a[n] = jnp.where(odd_lat, down, up)
        out_b[n] = jnp.where(odd_lat, up, down)

    def pack(n, read):
        for g in range(4):
            q = [read(4 * g + i) for i in range(4)]
            for i in range(3):
                last = pltpu.roll(q[3], 6 - 2 * i, 0)
                emit(n + g * 3 + i, jnp.where(sub >= 2, q[i], last), jnp.where(sub < 6, q[i], last))

    return emit, pack


def lon_first_kernel(
    ids, turned, zonal, merid_hbm, halo_a, halo_b, state_hbm, out_a, out_b, wind, weights, first, second, merid, surface, state, sems
):
    copies = load([(merid_hbm, merid), (zonal.at[pl.ds(0, 8)], surface)], sems)
    odd = (ids[1] & 1) == 1
    a, b = halo_a[16], halo_b[16]
    left, right = jnp.where(odd, a, b), jnp.where(odd, b, a)
    wind[0:8], wind[8:136], wind[136:144] = left, turned[16], right
    zonal_weights(wind, weights)
    sweep_columns(ids, 0, N1, turned, halo_a, halo_b, state, weights, first, second)
    store = pltpu.make_async_copy(state, state_hbm, sems.at[2])
    store.start()
    emit, pack = row_packer(ids, out_a, out_b)

    def body(t, carry):
        pack(12 * t, lambda k: state[t, 8 * k : 8 * k + 8, :])
        return carry

    lax.fori_loop(0, N1, body, 0)
    keep = jnp.logical_or(iota((8, 128), 0) < 7, ids[0] < 7)
    for c in copies:
        c.wait()
    pack(WIND, lambda k: jnp.where(keep, merid[k], 0.0))
    emit(WIND + 12, surface[...], surface[...])
    emit(WIND + 13, left, left)
    emit(WIND + 14, right, right)
    store.wait()


def lon_second_kernel(ids, turned, halo_a, halo_b, weights, state_hbm, out_a, out_b, first, second, state, sems):
    sweep_columns(ids, N1, N2, turned, halo_a, halo_b, state, weights, first, second)
    store = pltpu.make_async_copy(state, state_hbm, sems.at[0])
    store.start()
    _, pack = row_packer(ids, out_a, out_b)

    def body(t, carry):
        pack(12 * t, lambda k: state[t, 8 * k : 8 * k + 8, :])
        return carry

    lax.fori_loop(0, N2, body, 0)
    store.wait()


def row_reader(ids, halo_a, halo_b):
    odd_lat = (ids[0] & 1) == 1
    sub = iota((8, 128), 0)

    def message(n):
        a, b = halo_a[n], halo_b[n]
        return jnp.where(odd_lat, a, b), jnp.where(odd_lat, b, a)

    def four(n):
        got = [message(n + x) for x in range(3)]
        rolled = [[pltpu.roll(got[x][y], 2 + 2 * x, 0) for x in range(3)] for y in range(2)]
        low = jnp.where(sub < 4, rolled[0][0], jnp.where(sub < 6, rolled[0][1], rolled[0][2]))
        high = jnp.where(sub < 2, rolled[1][0], jnp.where(sub < 4, rolled[1][1], rolled[1][2]))
        return got + [(low, high)]

    return message, four


def sweep_rows(count, four, latw, wide, swept):
    def unpack(t, carry):
        for g in range(4):
            for x, (low, high) in enumerate(four(12 * t + 3 * g)):
                k = 4 * g + x
                wide[t, k, 0:8], wide[t, k, 16:24] = low, high
        return carry

    lax.fori_loop(0, count, unpack, 0, unroll=2)

    def level(k, carry):
        v = [latw[k, m] for m in range(13)]
        for t in range(count):
            q = v[0] * wide[t, k, 2:10]
            for m in range(1, 13):
                q = q + v[m] * wide[t, k, 2 + m : 10 + m]
            swept[t, pl.ds(pl.multiple_of(8 * k, 8), 8), :] = q
        return carry

    lax.fori_loop(0, 16, level, 0)


def mix(matrix, x):
    high = x.astype(BF16)
    low = (x - high.astype(F32)).astype(BF16)
    return (
        jnp.dot(matrix[0], high, preferred_element_type=F32)
        + jnp.dot(matrix[0], low, preferred_element_type=F32)
        + jnp.dot(matrix[1], high, preferred_element_type=F32)
    )


def parts(x):
    high = x.astype(BF16)
    return high, (x - high.astype(F32)).astype(BF16)


def rows_kernel(
    ids,
    state_hbm,
    merid_hbm,
    a_hbm,
    b_hbm,
    edge,
    mixing_hbm,
    grid_in,
    two_hbm,
    out_hbm,
    latw,
    matrix,
    emitted,
    two,
    swept,
    wide,
    wind,
    merid,
    halo_a,
    halo_b,
    mixing,
    lonw,
    grid,
    second,
    back,
    out,
    sems,
):
    copies = load(
        [(a_hbm, halo_a), (b_hbm, halo_b), (merid_hbm, merid), (mixing_hbm, mixing), (state_hbm, wide.at[:, :, pl.ds(8, 8), :])], sems
    )
    fetch = pltpu.make_async_copy(two_hbm, two, sems.at[5])
    fetch.start()
    sub = iota((8, 128), 0)
    keep = jnp.logical_or(sub < 7, ids[0] < 7)
    hi = lax.Precision.HIGHEST
    i, j = iota((128, 128), 0), iota((128, 128), 1)
    spread = jnp.where((j & 7) == i, 1.0, 0.0)

    def level_zero(n):
        wind[n] = jnp.dot(wind[n], spread, precision=hi, preferred_element_type=F32)
        zonal_weights(wind.at[n], lonw.at[n])

    wind[1] = edge[...]
    level_zero(1)
    copies[3].wait()
    order = jnp.where(((i & 7) * 16 + (i >> 3)) == j, 1.0, 0.0)
    by_level = jnp.dot(order, mixing[...], precision=hi, preferred_element_type=F32)
    expand = jnp.where((iota((16, 128), 1) >> 3) == iota((16, 128), 0), 1.0, 0.0)
    whole = jnp.dot(by_level, expand, precision=hi, preferred_element_type=F32)
    whole = jnp.where((i & 7) == (j & 7), whole, 0.0)
    matrix[...] = whole
    for c in copies[:3] + copies[4:]:
        c.wait()
    message, four = row_reader(ids, halo_a, halo_b)
    for g in range(4):
        for x, (low, high) in enumerate(four(WIND + 3 * g)):
            k = 4 * g + x
            v = lat_weights(jnp.where(keep, merid[k], 0.0), low, high, sub)
            for m in range(13):
                latw[k, m] = v[m]
    centre, left, right = message(WIND + 12), message(WIND + 13), message(WIND + 14)
    for n in (0, 2):
        m = n // 2
        wind[n, 0:8], wind[n, 136:144] = left[m], right[m]
        wind[n, 8:136] = jnp.concatenate([centre[m]] * 16, 0).T
        level_zero(n)
    for n in range(3):
        grid[n] = grid_in[n]
        zonal_steps_unrolled(lonw.at[n], grid.at[n], second.at[n])
    for n in range(3):
        x = grid[n, 8:136].T
        for t in range(16):
            back[t, 8 * n : 8 * n + 8] = x[8 * t : 8 * t + 8]
    for t in range(16):
        e = latw[0, 0] * back[t, 2:10]
        for m in range(1, 13):
            e = e + latw[0, m] * back[t, 2 + m : 10 + m]
        emitted[t] = e
    sweep_rows(N1, four, latw, wide, swept)
    split = parts(whole)
    for t in range(N1):
        swept[t, 0:8] = swept[t, 0:8] + emitted[t]
        out[t] = mix(split, swept[t])
    store = pltpu.make_async_copy(out, out_hbm.at[pl.ds(0, N1)], sems.at[0])
    store.start()
    fetch.wait()
    store.wait()


def last_kernel(ids, state, halo_a, halo_b, latw, matrix, emitted, _, out_hbm, swept, wide, out, sems):
    split = parts(matrix[...])
    for t in range(N2):
        for k in range(16):
            wide[t, k, 8:16] = state[t, 8 * k : 8 * k + 8]
    _, four = row_reader(ids, halo_a, halo_b)
    sweep_rows(N2, four, latw, wide, swept)
    half = N2 // 2
    stores = []
    for n, (first, count) in enumerate(((0, half), (half, N2 - half))):
        for t in range(first, first + count):
            swept[t, 0:8] = swept[t, 0:8] + emitted[N1 + t]
            out[t] = mix(split, swept[t])
        stores.append(
            pltpu.make_async_copy(out.at[pl.ds(first, count)], out_hbm.at[pl.ds(N1 + first, count)], sems.at[1 + n])
        )
        stores[-1].start()
    for c in stores:
        c.wait()


def scatter_kernel(got, grid, turned):
    sub = iota((8, 128), 0)
    spots = got[pl.ds(9, 128, stride=ROWS), :].T.astype(jnp.int32)
    row_of, col_of = spots >> 7, spots & 127

    def split(b):
        x = got[pl.ds(b, 128, stride=ROWS), :].T
        high = x.astype(BF16).astype(F32)
        return high, x - high

    def main(b):
        high, low = split(b)
        turned[0], turned[1] = high, low
        highs, lows, where = [], [], []
        target = iota((128, 128), 0)
        for s in range(8):
            here = row_of[8 * b + s : 8 * b + s + 1, :] == sub

            def rows(n):
                return jnp.concatenate(
                    [
                        jnp.where(here, jnp.broadcast_to(turned[n, 16 * s + t : 16 * s + t + 1, :], (8, 128)), 0.0)
                        for t in range(16)
                    ],
                    0,
                ).astype(BF16)

            highs.append(rows(0))
            lows.append(rows(1))
            where.append(jnp.where(col_of[8 * b + s : 8 * b + s + 1, :] == target, 1.0, 0.0).astype(BF16))
        where = jnp.concatenate(where, 1)
        return lax.dot_general(where, jnp.concatenate(highs, 1), NT, preferred_element_type=F32) + lax.dot_general(
            where, jnp.concatenate(lows, 1), NT, preferred_element_type=F32
        )

    expand = jnp.where((iota((32, 128), 0) & 15) == (iota((32, 128), 1) >> 3), 1.0, 0.0)
    diagonal = (iota((64, 128), 0) & 7) == (iota((64, 128), 1) & 7)

    def side(b, first):
        high, low = split(b)
        flux = jnp.concatenate(
            [jnp.concatenate([high[16 * s : 16 * s + 16], low[16 * s : 16 * s + 16]], 0) for s in range(8)], 1
        ).astype(BF16)
        key = (col_of - first) * 8 + row_of
        target = iota((64, 128), 0)
        where = jnp.concatenate(
            [jnp.where(key[8 * b + s : 8 * b + s + 1, :] == target, 1.0, 0.0) for s in range(8)], 1
        ).astype(BF16)
        sums = lax.dot_general(where, flux, NT, preferred_element_type=F32)
        sums = jnp.dot(sums, expand, precision=lax.Precision.HIGHEST, preferred_element_type=F32)
        sums = jnp.where(diagonal, sums, 0.0)
        return jnp.concatenate([jnp.sum(sums[8 * c : 8 * c + 8], 0, keepdims=True) for c in range(8)], 0)

    for n in range(3):
        grid[n, 0:8] = side(3 * n, 120)
        grid[n, 8:136] = main(3 * n + 1)
        grid[n, 136:144] = side(3 * n + 2, 0)


def call(kernel, ins, outs, scratch=(), kinds=None, copies=0, in_hbm=(), aliases=None, us=2):
    spec = {"s": pltpu.SMEM, "v": VM, "h": pltpu.HBM}
    rooms = [VM(x, F32) if isinstance(x, tuple) else x for x in scratch]
    if copies:
        rooms.append(pltpu.SemaphoreType.DMA((copies,)))
    return pl.pallas_call(
        kernel,
        out_shape=[pltpu.HBM(s, F32) if n in in_hbm else struct(s) for n, s in enumerate(outs)],
        in_specs=[pl.BlockSpec(memory_space=spec[x]) for x in kinds],
        out_specs=[pl.BlockSpec(memory_space=pltpu.HBM if n in in_hbm else VM) for n in range(len(outs))],
        scratch_shapes=rooms,
        compiler_params=PARAMS,
        cost_estimate=pl.CostEstimate(flops=0, bytes_accessed=int(us * 3.6e6), transcendentals=0),
        input_output_aliases=aliases or {},
    )(*[pltpu.with_memory_space_constraint(x, pltpu.HBM) if k == "h" else x for x, k in zip(ins, kinds)])


def struct(s):
    return jax.ShapeDtypeStruct(s, F32) if isinstance(s, tuple) else jax.ShapeDtypeStruct(s.shape, s.dtype)


def load(pairs, sems):
    copies = [pltpu.make_async_copy(x, y, sems.at[n]) for n, (x, y) in enumerate(pairs)]
    for c in copies:
        c.start()
    return copies


def on_device(
    features, land_tile, land_spot, w_in, b_in, w_mid, b_mid, w_out, tracers, zonal_wind, meridional_wind, mixing
):
    ids = jnp.stack([lax.axis_index("lat"), lax.axis_index("lon")]).astype(jnp.int32)
    shape = tracers.shape
    tracers = tracers.reshape(16, 128, 128)
    zonal = zonal_wind.reshape(128, 128)
    cells = features.shape[0]
    inputs = (
        features.T,
        land_tile.reshape(1, cells),
        land_spot.reshape(1, cells),
        w_in,
        b_in.reshape(1, -1),
        w_mid,
        b_mid.reshape(1, -1),
        w_out.T,
    )
    pack_a, pack_b, turned, *inputs = call(
        pack_kernel,
        (ids, tracers, zonal) + inputs,
        [(17, 8, 128), (17, 8, 128), (17, 128, 128)] + list(inputs),
        scratch=[(16, 128, 128), (128, 128)],
        us=2,
        kinds="shh" + "h" * 8,
        copies=13,
    )
    lon_a = [(i, i ^ 1) for i in range(16)]
    lon_b = [(i, (i + 1) % 16 if i & 1 else (i - 1) % 16) for i in range(16)]
    lat_a = [(i, i ^ 1) for i in range(8)]
    lat_b = [(i, i + 1 if i & 1 else i - 1) for i in range(1, 7)]
    halo_b = lax.ppermute(pack_b, "lon", lon_b)
    halo_a = lax.ppermute(pack_a, "lon", lon_a)
    (message,) = call(flux_kernel, inputs, [(128 * ROWS, 128)], us=3, kinds="v" * 8)
    halo_a, halo_b, message = lax.optimization_barrier((halo_a, halo_b, message))
    state_one, one_a, one_b, edge, weights = call(
        lon_first_kernel,
        (ids, turned, zonal, meridional_wind, halo_a, halo_b),
        [(N1, 128, 128), (MSG1, 8, 128), (MSG1, 8, 128), (144, 128), (7, 136, 128)],
        scratch=[(N1, 144, 128), (N1, 136, 128), (16, 8, 128), (8, 128), (N1, 128, 128)],
        us=3,
        kinds="svhhvv",
        copies=3,
        in_hbm=(0,),
    )
    ones_b = lax.ppermute(one_b, "lat", lat_b)
    ones_a = lax.ppermute(one_a, "lat", lat_a)
    got = lax.all_to_all(
        message.reshape(128, 1, ROWS * 128), ("lat", "lon"), split_axis=0, concat_axis=0, tiled=True
    ).reshape(128 * ROWS, 128)
    state_two, two_a, two_b = call(
        lon_second_kernel,
        (ids, turned, halo_a, halo_b, weights),
        [(N2, 128, 128), (MSG2, 8, 128), (MSG2, 8, 128)],
        scratch=[(N2, 144, 128), (N2, 136, 128), (N2, 128, 128)],
        us=3,
        kinds="svvvv",
        copies=1,
        in_hbm=(0,),
    )
    twos_a = lax.ppermute(two_a, "lat", lat_a)
    twos_b = lax.ppermute(two_b, "lat", lat_b)
    (grid,) = call(scatter_kernel, (got,), [(3, 144, 128)], scratch=[(2, 128, 128)], kinds="v")
    ones_b, ones_a, grid = lax.optimization_barrier((ones_b, ones_a, grid))
    out, latw, matrix, emitted, state_two = call(
        rows_kernel,
        (ids, state_one.reshape(N1, 16, 8, 128), meridional_wind, ones_a, ones_b, edge, mixing.reshape(128, 16), grid, state_two),
        [(16, 128, 128), (16, 13, 8, 128), (128, 128), (16, 8, 128), (N2, 128, 128)],
        scratch=[
            (N1, 128, 128),
            (N1, 16, 24, 128),
            (3, 144, 128),
            (16, 8, 128),
            (MSG1, 8, 128),
            (MSG1, 8, 128),
            (128, 16),
            (3, 7, 136, 128),
            (3, 144, 128),
            (3, 136, 128),
            (16, 24, 128),
            (N1, 128, 128),
        ],
        us=5,
        kinds="shhhhvhvh",
        copies=6,
        in_hbm=(0,),
    )
    (out,) = call(
        last_kernel,
        (ids, state_two, twos_a, twos_b, latw, matrix, emitted, out),
        [(16, 128, 128)],
        scratch=[
            (N2, 128, 128),
            (N2, 16, 24, 128),
            (N2, 128, 128),
        ],
        us=4,
        kinds="svvvvvvh",
        copies=3,
        in_hbm=(0,),
        aliases={7: 0},
    )
    return out.reshape(shape)


def solution(mesh):
    placed = (
        P(("lat", "lon"), None),
        P(("lat", "lon"), None),
        P(("lat", "lon")),
        P(),
        P(),
        P(),
        P(),
        P(),
        P(None, None, "lat", "lon"),
        P(None, "lat", "lon"),
        P(None, "lat", "lon"),
        P("lat", None, None),
    )
    return jax.shard_map(
        on_device,
        mesh=mesh,
        in_specs=placed,
        out_specs=P(None, None, "lat", "lon"),
        check_vma=False,
    )
```
